128 devices in a mesh: lat: 16 (over z, y_hi, core), lon: 8 (over y_lo, x).
Axes of the slice: x: 4, y: 4 (y_hi: 2, y_lo: 2; y = y_hi * 2 + y_lo), z: 4, core: 2. Of those that a mesh axis runs over, the one named last changes fastest.
Arguments:
- fields: float32 [6, 32, 256, 2880], P(None, None, 'lat', 'lon'), may hold values from -6 to 6
- inv_cos: float32 [256], P('lat'), may hold values from 0.9 to 8.8
- coupling_lon: float32 [6, 6], replicated, may hold values from -0.4 to 0.4
- coupling_lat: float32 [6, 6], replicated, may hold values from -1.5 to 1.5
- polar_rows: int32 [56], replicated, may hold values from 0 to 255, as said below
- bands: int32 [56], replicated, may hold values from 32 to 1024, as said below
Outputs:
- smoothed_fields: float32 [6, 32, 256, 2880], P(None, None, 'lat', 'lon')
The draws below stay inside these ranges and needn't reach their ends.
Inputs may be any that keep to these rules, and one draw needn't show every extreme that they name: `polar_rows`: ascending and distinct; each of the first 2 and the last 2 blocks of 16 rows holds exactly 14 of them, rows 0 and 255 are always listed, and no other row is listed. `bands`: the band width of the row at the same position of polar_rows: with d the row's distance from its nearest end row (0 or 255) and e the largest such distance among the listed rows at that end, it is 32 + ((992) d) // e.
All inputs are finite; a program needn't handle non-finite values.
Results may differ from the reference program's by a relative error of at most 0.00005.
Values sent between devices are 32-bit elements; how exact they have to be, the bound alone decides.
A program may use at most 128 MiB of HBM per device.

```python
import math
import jax
import jax.numpy as jnp
from jax import lax

F = 6
NLON = 2880
LEV = 32
LAT_DEV = 16
KMAX = 1024
KMIN = 32
NPOL = 2
CAP = 14
NLAT = 256
N_LAT = 16


def listing(key):
    tiles = jnp.concatenate([jnp.arange(NPOL, dtype=jnp.int32), N_LAT - NPOL + jnp.arange(NPOL, dtype=jnp.int32)])
    keys = jax.random.split(jax.random.fold_in(key, 11), 2 * NPOL)
    lifts = jax.random.randint(jax.random.fold_in(key, 13), (2 * NPOL,), 0, 2).astype(jnp.int32)
    lifts = lifts.at[0].set(1).at[2 * NPOL - 1].set(0)
    offsets = jnp.arange(LAT_DEV, dtype=jnp.int32)

    def one_block(single, lift):
        order = jax.random.permutation(single, LAT_DEV - 1).astype(jnp.int32)
        dropped = order[:LAT_DEV - CAP] + lift
        gone = jnp.sum((offsets[:, None] == dropped[None, :]).astype(jnp.int32), axis=1)
        ranking = jnp.where(gone > 0, LAT_DEV + offsets, offsets)
        return jnp.argsort(ranking, stable=True)[:CAP].astype(jnp.int32)
    picks = jax.vmap(one_block)(keys, lifts)
    return (tiles[:, None] * LAT_DEV + picks).reshape(-1).astype(jnp.int32)


def draw_polar_rows(key, part):
    return listing(key)


def draw_bands(key, part):
    rows = listing(key)
    half = NPOL * CAP
    north = rows[:half]
    south = NLAT - 1 - rows[half:]
    far_north = jnp.maximum(jnp.max(north), 1)
    far_south = jnp.maximum(jnp.max(south), 1)
    band_north = KMIN + (KMAX - KMIN) * north // far_north
    band_south = KMIN + (KMAX - KMIN) * south // far_south
    return jnp.concatenate([band_north, band_south]).astype(jnp.int32)


def draw_inv_cos(key, part):
    rows = jnp.arange(NLAT, dtype=jnp.float32)
    middle = (NLAT - 1) / 2.0
    spread_pos = jnp.abs(rows - middle) / middle
    base = 1.0 + 7.0 * spread_pos * spread_pos * spread_pos
    jitter = jax.random.uniform(jax.random.fold_in(key, 31), (NLAT,), jnp.float32, 0.95, 1.05)
    return (base * jitter).astype(jnp.float32)


def steps_of(own_key, extent, pieces, least, high):
    def one(axis_at, parts):
        steps = jax.random.uniform(jax.random.fold_in(jax.random.fold_in(own_key, 6), axis_at), (parts,), jnp.float32, least / len(pieces), high / len(pieces))
        return jnp.repeat(jnp.exp(steps), extent[axis_at] // parts).reshape((-1,) + (1,) * (len(extent) - axis_at - 1))

    factor_of = one(*pieces[0])
    for cut in pieces[1:]:
        factor_of = factor_of * one(*cut)
    return factor_of


def noise(rng, dims, scale, bound, cuts=(), held_as=jnp.bfloat16):
    loudness = steps_of(rng, dims, cuts, -0.22, 0.18) if cuts else 1.0
    values = jax.random.normal(rng, dims, jnp.float32) * scale * loudness
    return jnp.minimum(jnp.maximum(values, -bound), bound).astype(held_as)


def setup_inputs(seed: int = 0) -> dict:
    key_list = jax.random.split(jax.random.key(seed), 7)
    fields = noise(key_list[0], (F, LEV, NLAT, NLON), 1.0, 6.0, ((2, 16), (3, 8)), jnp.float32)
    inv_cos = draw_inv_cos(jax.random.fold_in(key_list[6], 71), 0)
    coupling_lon = noise(key_list[2], (F, F), 0.08, 0.4, (), jnp.float32)
    coupling_lat = noise(key_list[3], (F, F), 0.3, 1.5, (), jnp.float32)
    polar_rows = draw_polar_rows(jax.random.fold_in(key_list[6], 71), 0)
    bands = draw_bands(jax.random.fold_in(key_list[6], 71), 0)
    return dict(fields=fields, inv_cos=inv_cos, coupling_lon=coupling_lon, coupling_lat=coupling_lat, polar_rows=polar_rows, bands=bands)


def difference(padded, axis, count):
    def shifted(offset):
        return lax.slice_in_dim(padded, 3 + offset, 3 + offset + count, axis=axis)
    return (45.0 * (shifted(1) - shifted(-1)) - 9.0 * (shifted(2) - shifted(-2)) + (shifted(3) - shifted(-3))) / 60.0


def fourier_table(length, modes):
    cells = jnp.arange(length, dtype=jnp.int32)
    waves = jnp.arange(modes, dtype=jnp.int32)
    phase = ((cells[:, None] * waves[None, :]) % length).astype(jnp.float32) * (2.0 * math.pi / length)
    return jnp.concatenate([jnp.cos(phase), jnp.sin(phase)], axis=1)


def mode_weights(band_each, modes, length):
    columns = jnp.arange(2 * modes, dtype=jnp.int32) % modes
    keep = columns[None, :] < band_each[:, None]
    factor = jnp.where(columns == 0, 1.0, 2.0) / length
    return jnp.where(keep, factor[None, :], 0.0).astype(jnp.float32)


def advance(fields, padded_lat, padded_lon, inv_cos, coupling_lon, coupling_lat):
    along_lat = difference(padded_lat, 2, fields.shape[2])
    along_lon = difference(padded_lon, 3, fields.shape[3]) * inv_cos[None, None, :, None]
    change = jnp.einsum("fg,glrn->flrn", coupling_lon, along_lon, precision=lax.Precision.HIGHEST)
    change = change + jnp.einsum("fg,glrn->flrn", coupling_lat, along_lat, precision=lax.Precision.HIGHEST)
    return fields + change


def reference(fields, inv_cos, coupling_lon, coupling_lat, polar_rows, bands):
    padded_lat = jnp.pad(fields, ((0, 0), (0, 0), (3, 3), (0, 0)))
    padded_lon = jnp.concatenate([fields[..., -3:], fields, fields[..., :3]], axis=3)
    predicted = advance(fields, padded_lat, padded_lon, inv_cos, coupling_lon, coupling_lat)
    listed = predicted[:, :, polar_rows, :]
    table = fourier_table(NLON, KMAX)
    spectra = jnp.einsum("flin,nk->flik", listed, table, precision=lax.Precision.HIGHEST)
    weights = mode_weights(bands, KMAX, NLON)
    filtered = jnp.einsum("flik,nk->flin", spectra * weights[None, None], table, precision=lax.Precision.HIGHEST)
    return predicted.at[:, :, polar_rows, :].set(filtered)
```

```python
import math

import jax
import jax.numpy as jnp
import ml_dtypes
import numpy as np
from jax import lax
from jax.experimental import pallas as pl
from jax.experimental.pallas import tpu as pltpu
from jax.sharding import PartitionSpec as P

MESH = pl.DeviceIdType.MESH
F, LEV, ROWS, CELLS, WIDE = 6, 32, 16, 360, 384
PARTS, LENGTH, KMAX, CAP = 8, 2880, 1024, 14
GROUPS, QUADS = LEV // 8, LEV // 8 * F
SLOT = QUADS
UNITS = CAP * SLOT
REL, OWN = 10, 11
UP0, DOWN0, OWN0 = 0, PARTS * REL, 2 * PARTS * REL
BLOCK = 12
BATCH = 8 * BLOCK
HALF = 1.0 / math.sqrt(2.0)


def tables():
    cells = np.arange(CELLS, dtype=np.int64)

    def angles(waves):
        return 2.0 * np.pi * ((cells[:, None] * waves[None, :]) % LENGTH) / LENGTH

    def halves(table):
        wide = np.asarray(table, np.float64)
        head = wide.astype(ml_dtypes.bfloat16)
        return head, (wide - head.astype(np.float64)).astype(ml_dtypes.bfloat16)

    pair = np.zeros((3, 2 * WIDE, 512))
    single = np.zeros((2, WIDE, 256))
    waves_pair = np.zeros((3, 1, 512), np.int32)
    waves_single = np.zeros((2, 1, 256), np.int32)
    for kind in (1, 2, 3):
        waves = kind + 8 * np.arange(-128, 128)
        cos, sin = np.cos(angles(waves)), np.sin(angles(waves))
        pair[kind - 1, :CELLS, :256] = cos
        pair[kind - 1, :CELLS, 256:] = -sin
        pair[kind - 1, WIDE : WIDE + CELLS, :256] = sin
        pair[kind - 1, WIDE : WIDE + CELLS, 256:] = cos
        waves_pair[kind - 1, 0] = np.concatenate([np.abs(waves)] * 2)
    for at, kind in enumerate((0, 4)):
        waves = kind + 8 * np.arange(128)
        single[at, :CELLS, :128] = np.cos(angles(waves))
        single[at, :CELLS, 128:] = -np.sin(angles(waves))
        waves_single[at, 0] = np.concatenate([waves] * 2)
    return (*halves(pair), *halves(single), waves_pair, waves_single)


def kernel(
    fields, inv_cos, c_lon, c_lat, polar_rows, bands, pair_hi, pair_lo, one_hi, one_lo, waves_pair, waves_one,
    out,
    grid, lon_out, lon_in, pred, slots, relay, pieces, result, back, spec, t_ph, t_pl, t_oh, t_ol, turned,
    tab_sem, lon_ss, lon_rs, lat_ss, lat_rs, help_ss, help_rs, own_ss, own_rs, self_sem, ret_ss, ret_rs, ret_self,
):
    t, i = lax.axis_index("lat"), lax.axis_index("lon")
    north, south = t < 2, t >= 14
    polar = north | south
    up = (t >= 2) & (t < 6)
    down = (t >= 10) & (t < 14)
    helper = up | down
    host = jnp.where(polar, t, jnp.where(up, lax.rem(t + 12, 16), lax.rem(t + 4, 16)))
    flip = host >= 14
    first = jnp.where(host < 2, host, jnp.where(flip, host - 12, 0)) * CAP

    loads = [
        pltpu.make_async_copy(src, dst, tab_sem.at[n])
        for n, (src, dst) in enumerate(((pair_hi, t_ph), (pair_lo, t_pl), (one_hi, t_oh), (one_lo, t_ol)))
    ]
    for load in loads:
        load.start()

    barrier = pltpu.get_barrier_semaphore()

    def greet(lat, lon):
        pl.semaphore_signal(barrier, inc=1, device_id=(lat, lon), device_id_type=MESH)

    for k in range(1, PARTS):
        greet(t, lax.rem(i + k, PARTS))

    @pl.when(t > 0)
    def _():
        greet(t - 1, i)

    @pl.when(t < 15)
    def _():
        greet(t + 1, i)

    @pl.when(polar)
    def _():
        for k in range(PARTS):
            greet(lax.rem(t + 4, 16), k)
            greet(lax.rem(t + 12, 16), k)

    @pl.when(helper)
    def _():
        for k in range(PARTS):
            greet(host, k)

    lane = lax.broadcasted_iota(jnp.int32, (8, 128), 1)

    def turn(at, _):
        f, g = at // GROUPS, lax.rem(at, GROUPS)
        base = pl.multiple_of(at * 128, 128)
        turned[0, pl.ds(base, 128), :] = fields[pl.ds(base, 128), 0:128]
        turned[1, pl.ds(base, 128), :] = fields[pl.ds(base, 128), 128:256]
        turned[2, pl.ds(base, 128), 0 : CELLS - 256] = fields[pl.ds(base, 128), 256:CELLS]
        for r in range(ROWS):
            for c in range(3):
                tile = turned[c, pl.ds(base + r, 8, stride=ROWS), :]
                if c == 2:
                    tile = jnp.where(lane < CELLS - 256, tile, 0.0)
                grid[r + 3, g, f, :, 128 * c : 128 * (c + 1)] = tile
        return 0

    lax.fori_loop(0, QUADS, turn, 0)

    def pack(g, _):
        for pair in range(F // 2):

            def add(r, sums):
                low, high = sums
                for odd in range(2):
                    k = odd * 16 + r
                    mine = lane // 4 == k
                    head = grid[r + 3, g, 2 * pair + odd, :, 0:128]
                    tail = grid[r + 3, g, 2 * pair + odd, :, 256:WIDE]
                    low = jnp.where(mine, pltpu.roll(head, 4 * k, axis=1), low)
                    high = jnp.where(mine, pltpu.roll(tail, lax.rem(4 * k + 128 - 101, 128), axis=1), high)
                return low, high

            zero = jnp.zeros((8, 128), jnp.float32)
            low, high = lax.fori_loop(0, ROWS, add, (zero, zero))
            lon_out[0, g, pair] = low
            lon_out[1, g, pair] = high
        return 0

    lax.fori_loop(0, GROUPS, pack, 0)

    edge = jnp.where(t > 0, 1, 0) + jnp.where(t < 15, 1, 0)
    pl.semaphore_wait(barrier, PARTS - 1 + edge + jnp.where(polar, 2 * PARTS, 0) + jnp.where(helper, PARTS, 0))

    lon_copies = [
        pltpu.make_async_remote_copy(
            src_ref=lon_out.at[side], dst_ref=lon_in.at[side], send_sem=lon_ss.at[side], recv_sem=lon_rs.at[side],
            device_id=(t, lax.rem(i + shift, PARTS)), device_id_type=MESH,
        )
        for side, shift in ((0, PARTS - 1), (1, 1))
    ]
    for copy in lon_copies:
        copy.start()
    south_copy = pltpu.make_async_remote_copy(
        src_ref=grid.at[pl.ds(16, 3)], dst_ref=grid.at[pl.ds(0, 3)], send_sem=lat_ss.at[0], recv_sem=lat_rs.at[0],
        device_id=(jnp.minimum(t + 1, 15), i), device_id_type=MESH,
    )
    north_copy = pltpu.make_async_remote_copy(
        src_ref=grid.at[pl.ds(3, 3)], dst_ref=grid.at[pl.ds(19, 3)], send_sem=lat_ss.at[1], recv_sem=lat_rs.at[1],
        device_id=(jnp.maximum(t - 1, 0), i), device_id_type=MESH,
    )

    @pl.when(t < 15)
    def _():
        south_copy.start()

    @pl.when(t > 0)
    def _():
        north_copy.start()

    def clear(row0):
        def one(r, _):
            for g in range(GROUPS):
                for f in range(F):
                    grid[row0 + r, g, f] = jnp.zeros((8, WIDE), jnp.float32)
            return 0

        lax.fori_loop(0, 3, one, 0)

    @pl.when(t == 0)
    def _():
        clear(0)

    @pl.when(t == 15)
    def _():
        clear(19)

    for copy in lon_copies:
        copy.wait_recv()

    def wait_above():
        @pl.when(t > 0)
        def _():
            south_copy.wait_recv()

    def wait_below():
        @pl.when(t < 15)
        def _():
            north_copy.wait_recv()

    def step(at, _):
        n, g = at // GROUPS, lax.rem(at, GROUPS)
        r = jnp.where(flip, ROWS - 1 - n, n)
        scale = inv_cos[r] * (1.0 / 60.0)
        centre, along_lon, along_lat = [], [], []
        for f in range(F):
            k = (f % 2) * 16 + r
            east = pltpu.roll(lon_in[0, g, f // 2], lax.rem(104 + 128 - 4 * k, 128), axis=1)
            west = pltpu.roll(lon_in[1, g, f // 2], lax.rem(125 + 128 - 4 * k, 128), axis=1)
            mid = grid[r + 3, g, f]
            halo = jnp.where((lane >= 104) & (lane < 107), east, jnp.where(lane >= 125, west, 0.0))
            cells = jnp.concatenate([mid[:, :256], mid[:, 256:] + halo], axis=1)
            centre.append(mid)

            def at_cell(d):
                return pltpu.roll(cells, (WIDE - d) % WIDE, axis=1)

            along_lon.append(
                (45.0 * (at_cell(1) - at_cell(-1)) - 9.0 * (at_cell(2) - at_cell(-2)) + (at_cell(3) - at_cell(-3)))
                * scale
            )

            def at_row(d):
                return grid[r + 3 + d, g, f]

            along_lat.append(
                (45.0 * (at_row(1) - at_row(-1)) - 9.0 * (at_row(2) - at_row(-2)) + (at_row(3) - at_row(-3)))
                * (1.0 / 60.0)
            )
        for f in range(F):
            total = centre[f]
            for h in range(F):
                total = total + c_lon[f * F + h] * along_lon[h] + c_lat[f * F + h] * along_lat[h]
            pred[r, g * F + f] = jnp.where(lax.broadcasted_iota(jnp.int32, (8, WIDE), 1) < CELLS, total, 0.0)

        @pl.when(polar & (g == GROUPS - 1) & (n >= 2))
        def _():
            s = jnp.where(flip, CAP - 1 - (n - 2), n - 2)
            row = jnp.clip(polar_rows[first + s] - t * ROWS, 0, ROWS - 1)
            for q in range(SLOT):
                slots[(n - 2) * SLOT + q] = pred[row, q]

        return 0

    def rows_from(lo, hi):
        lax.fori_loop(lo * GROUPS, hi * GROUPS, step, 0)

    def helper_send(which, j):
        base = (UP0, DOWN0)[which]
        return pltpu.make_async_remote_copy(
            src_ref=slots.at[pl.ds(base + j * REL, REL)], dst_ref=relay.at[j],
            send_sem=help_ss.at[which, j], recv_sem=help_rs.at[j],
            device_id=(lax.rem(t + (4, 12)[which], 16), i), device_id_type=MESH,
        )

    def own_send(block, p, j):
        return pltpu.make_async_remote_copy(
            src_ref=slots.at[pl.ds(OWN0 + block * PARTS * OWN + j * OWN, OWN)],
            dst_ref=pieces.at[block, p, pl.ds(0, OWN)],
            send_sem=own_ss.at[block, j], recv_sem=own_rs.at[block, p],
            device_id=(t, j), device_id_type=MESH,
        )

    def own_local(block):
        return pltpu.make_async_copy(
            slots.at[pl.ds(OWN0 + block * PARTS * OWN + i * OWN, OWN)],
            pieces.at[block, i, pl.ds(0, OWN)], self_sem.at[block],
        )

    def relay_send(p, j):
        return pltpu.make_async_remote_copy(
            src_ref=relay.at[j], dst_ref=pieces.at[0, p, pl.ds(0, REL)],
            send_sem=own_ss.at[0, j], recv_sem=own_rs.at[0, p],
            device_id=(t, j), device_id_type=MESH,
        )

    def relay_local():
        return pltpu.make_async_copy(relay.at[i], pieces.at[0, i, pl.ds(0, REL)], self_sem.at[0])

    @pl.when(polar & jnp.logical_not(flip))
    def _():
        wait_above()

    @pl.when(polar & flip)
    def _():
        wait_below()

    rows_from(jnp.where(polar, 0, 3), 6)

    def others(act):
        def one(k, _):
            act(lax.rem(i + k, PARTS))
            return 0

        lax.fori_loop(1, PARTS, one, 0)

    def everyone(act):
        def one(k, _):
            act(lax.rem(i + k, PARTS))
            return 0

        lax.fori_loop(1, PARTS + 1, one, 0)

    @pl.when(polar)
    def _():
        everyone(lambda j: helper_send(0, j).start())

    rows_from(6, 9)

    @pl.when(polar)
    def _():
        everyone(lambda j: helper_send(1, j).start())

    rows_from(9, 13)

    @pl.when(polar)
    def _():
        others(lambda j: own_send(0, i, j).start())
        own_local(0).start()

    @pl.when(helper)
    def _():
        def pass_on(j):
            helper_send(0, j).wait_recv()
            relay_send(i, j).start()

        others(pass_on)
        helper_send(0, i).wait_recv()
        relay_local().start()

    @pl.when(polar & jnp.logical_not(flip))
    def _():
        wait_below()

    @pl.when(polar & flip)
    def _():
        wait_above()

    @pl.when(jnp.logical_not(polar))
    def _():
        wait_above()
        wait_below()

    rows_from(0, jnp.where(polar, 0, 3))
    rows_from(13, 16)

    @pl.when(polar)
    def _():
        others(lambda j: own_send(1, i, j).start())
        own_local(1).start()

    for load in loads:
        load.wait()

    def ret_own(block, p, j):
        return pltpu.make_async_remote_copy(
            src_ref=result.at[block, p, pl.ds(0, OWN)],
            dst_ref=back.at[pl.ds(OWN0 + block * PARTS * OWN + j * OWN, OWN)],
            send_sem=ret_ss.at[block, p], recv_sem=ret_rs.at[block * PARTS + j],
            device_id=(t, p), device_id_type=MESH,
        )

    def ret_own_local(block):
        return pltpu.make_async_copy(
            result.at[block, i, pl.ds(0, OWN)],
            back.at[pl.ds(OWN0 + block * PARTS * OWN + i * OWN, OWN)], ret_self.at[block],
        )

    def ret_help(which, p, j):
        return pltpu.make_async_remote_copy(
            src_ref=result.at[0, p, pl.ds(0, REL)],
            dst_ref=back.at[pl.ds(which * PARTS * REL + j * REL, REL)],
            send_sem=ret_ss.at[0, p], recv_sem=ret_rs.at[(2 + which) * PARTS + j],
            device_id=(host, p), device_id_type=MESH,
        )

    def matmul(wide, head, tail, back_again):
        top = wide.astype(jnp.bfloat16)
        low = (wide - top.astype(jnp.float32)).astype(jnp.bfloat16)
        dims = (((1,), (1 if back_again else 0,)), ((), ()))
        both = lax.dot_general(
            jnp.concatenate([top, low], axis=0), head, dims, preferred_element_type=jnp.float32
        )
        cross = lax.dot_general(top, tail, dims, preferred_element_type=jnp.float32)
        return both[:BATCH] + (both[BATCH:] + cross)

    def band_column(block):
        start = jnp.where(
            polar,
            OWN0 + block * PARTS * OWN + i * OWN,
            jnp.where(up, UP0 + i * REL, DOWN0 + i * REL),
        )
        unit_of = lax.broadcasted_iota(jnp.int32, (BATCH, 1), 0) // 8
        column = jnp.zeros((BATCH, 1), jnp.int32)
        for n in range(BLOCK):
            s = jnp.minimum((start + n) // SLOT, CAP - 1)
            s = jnp.where(flip, CAP - 1 - s, s)
            column = jnp.where(unit_of == n, bands[first + s], column)
        return column

    def filter_block(block, _):
        @pl.when(polar)
        def _():
            others(lambda p: own_send(block, p, i).wait_recv())
            own_local(block).wait()

        @pl.when(helper)
        def _():
            others(lambda p: relay_send(p, i).wait_recv())
            relay_local().wait()

        def forward(n, _):
            x = [pieces[block, p, n] for p in range(PARTS)]
            e = [x[p] + x[p + 4] for p in range(4)]
            d = [x[p] - x[p + 4] for p in range(4)]
            here = pl.ds(pl.multiple_of(n * 8, 8), 8)
            minus, plus = HALF * (d[1] - d[3]), HALF * (d[1] + d[3])
            parts = (
                d[0] + minus, -plus - d[2],
                e[0] - e[2], e[3] - e[1],
                d[0] - minus, d[2] - plus,
                (e[0] + e[2]) + (e[1] + e[3]), (e[0] + e[2]) - (e[1] + e[3]),
            )
            for m, part in enumerate(parts):
                spec[here, m * WIDE : (m + 1) * WIDE] = part
            return 0

        lax.fori_loop(0, BLOCK, forward, 0)
        column = band_column(block)
        for m in range(3):
            here = slice(m * 2 * WIDE, (m + 1) * 2 * WIDE)
            waves = matmul(spec[:, here], t_ph[m], t_pl[m], False)
            waves = jnp.where(waves_pair[m] < column, waves * (2.0 / LENGTH), 0.0)
            spec[:, here] = matmul(waves, t_ph[m], t_pl[m], True)
        for m in range(2):
            here = slice((6 + m) * WIDE, (7 + m) * WIDE)
            waves = matmul(spec[:, here], t_oh[m], t_ol[m], False)
            factor = jnp.where(waves_one[m] == 0, 1.0 / LENGTH, 2.0 / LENGTH)
            waves = jnp.where(waves_one[m] < column, waves * factor, 0.0)
            spec[:, here] = matmul(waves, t_oh[m], t_ol[m], True)

        def inverse(n, _):
            here = pl.ds(pl.multiple_of(n * 8, 8), 8)
            r1, i1, r2, i2, r3, i3, z0, z4 = (spec[here, m * WIDE : (m + 1) * WIDE] for m in range(8))
            even, odd = z0 + z4, z0 - z4
            a, b = even + r2, even - r2
            c, d = odd - i2, odd + i2
            rr, ii = r1 + r3, i1 - i3
            u = HALF * ((r1 - r3) - (i1 + i3))
            v = HALF * ((r3 - r1) - (i1 + i3))
            outs = (a + rr, c + u, b - ii, d + v, a - rr, c - u, b + ii, d - v)
            for p, value in enumerate(outs):
                result[block, p, n] = value
            return 0

        lax.fori_loop(0, BLOCK, inverse, 0)

        @pl.when(polar)
        def _():
            others(lambda p: ret_own(block, p, i).start())
            ret_own_local(block).start()

        @pl.when(up)
        def _():
            everyone(lambda p: ret_help(0, p, i).start())

        @pl.when(down)
        def _():
            everyone(lambda p: ret_help(1, p, i).start())

        return 0

    lax.fori_loop(0, jnp.where(polar, 2, jnp.where(helper, 1, 0)), filter_block, 0)

    for copy in lon_copies:
        copy.wait_send()

    @pl.when(t < 15)
    def _():
        south_copy.wait_send()

    @pl.when(t > 0)
    def _():
        north_copy.wait_send()

    def put(value_of):
        def one(at, _):
            f, g = at // GROUPS, lax.rem(at, GROUPS)
            base = pl.multiple_of(at * 128, 128)
            for r in range(ROWS):
                value = value_of(r, g * F + f)
                for c in range(3):
                    turned[c, pl.ds(base + r, 8, stride=ROWS), :] = value[:, 128 * c : 128 * (c + 1)]
            out[pl.ds(base, 128), 0:128] = turned[0, pl.ds(base, 128), :]
            out[pl.ds(base, 128), 128:256] = turned[1, pl.ds(base, 128), :]
            out[pl.ds(base, 128), 256:CELLS] = turned[2, pl.ds(base, 128), 0 : CELLS - 256]
            return 0

        lax.fori_loop(0, QUADS, one, 0)

    @pl.when(jnp.logical_not(polar))
    def _():
        put(lambda r, q: pred[r, q])

    @pl.when(helper)
    def _():
        others(lambda j: relay_send(i, j).wait_send())
        everyone(lambda p: ret_help(0, p, i).wait_send())

    @pl.when(polar)
    def _():
        for which in range(2):
            everyone(lambda j: helper_send(which, j).wait_send())
        for block in range(2):
            others(lambda j: own_send(block, i, j).wait_send())
            others(lambda p: ret_own(block, p, i).wait_send())
            others(lambda j: ret_own(block, i, j).wait_recv())
            ret_own_local(block).wait()
        for which in range(2):
            everyone(lambda j: ret_help(which, i, j).wait_recv())

        place = []
        for r in range(ROWS):
            before, hit = 0, 0
            for s in range(CAP):
                row = polar_rows[first + s] - t * ROWS
                before = before + jnp.where(row < r, 1, 0)
                hit = hit + jnp.where(row == r, 1, 0)
            s = jnp.minimum(before, CAP - 1)
            place.append((hit > 0, jnp.where(flip, CAP - 1 - s, s) * SLOT))
        put(lambda r, q: jnp.where(place[r][0], back[place[r][1] + q], pred[r, q]))


def local(fields, inv_cos, coupling_lon, coupling_lat, polar_rows, bands):
    smem, vmem, anywhere = (pl.BlockSpec(memory_space=space) for space in (pltpu.SMEM, pltpu.VMEM, pl.ANY))
    dma = pltpu.SemaphoreType.DMA
    pair_hi, pair_lo, one_hi, one_lo, waves_pair, waves_one = tables()
    f32, bf16 = jnp.float32, jnp.bfloat16
    out = pl.pallas_call(
        kernel,
        out_shape=jax.ShapeDtypeStruct((F * LEV * ROWS, CELLS), f32),
        in_specs=[vmem] + [smem] * 5 + [anywhere] * 4 + [vmem] * 2,
        out_specs=vmem,
        scratch_shapes=[
            pltpu.VMEM((ROWS + 6, GROUPS, F, 8, WIDE), f32),
            pltpu.VMEM((2, GROUPS, F // 2, 8, 128), f32),
            pltpu.VMEM((2, GROUPS, F // 2, 8, 128), f32),
            pltpu.VMEM((ROWS, QUADS, 8, WIDE), f32),
            pltpu.VMEM((UNITS, 8, WIDE), f32),
            pltpu.VMEM((PARTS, REL, 8, WIDE), f32),
            pltpu.VMEM((2, PARTS, BLOCK, 8, WIDE), f32),
            pltpu.VMEM((2, PARTS, BLOCK, 8, WIDE), f32),
            pltpu.VMEM((UNITS, 8, WIDE), f32),
            pltpu.VMEM((BATCH, 8 * WIDE), f32),
            pltpu.VMEM((3, 2 * WIDE, 512), bf16),
            pltpu.VMEM((3, 2 * WIDE, 512), bf16),
            pltpu.VMEM((2, WIDE, 256), bf16),
            pltpu.VMEM((2, WIDE, 256), bf16),
            pltpu.VMEM((3, F * LEV * ROWS, 128), f32),
            dma((4,)),
            dma((2,)), dma((2,)), dma((2,)), dma((2,)),
            dma((2, PARTS)), dma((PARTS,)),
            dma((2, PARTS)), dma((2, PARTS)), dma((2,)),
            dma((2, PARTS)), dma((4 * PARTS,)), dma((2,)),
        ],
        compiler_params=pltpu.CompilerParams(
            collective_id=0, has_side_effects=True, vmem_limit_bytes=60 * 2**20
        ),
    )(
        fields.reshape(F * LEV * ROWS, CELLS),
        inv_cos,
        coupling_lon.reshape(-1),
        coupling_lat.reshape(-1),
        polar_rows,
        bands,
        jnp.asarray(pair_hi), jnp.asarray(pair_lo), jnp.asarray(one_hi), jnp.asarray(one_lo),
        jnp.asarray(waves_pair), jnp.asarray(waves_one),
    )
    return out.reshape(F, LEV, ROWS, CELLS)


def solution(mesh):
    return jax.shard_map(
        local,
        mesh=mesh,
        in_specs=(P(None, None, "lat", "lon"), P("lat"), P(), P(), P(), P()),
        out_specs=P(None, None, "lat", "lon"),
        check_vma=False,
    )
```

```python
import functools
import math

import jax
import jax.numpy as jnp
import ml_dtypes
import numpy as np
from jax import lax
from jax.experimental import pallas as pl
from jax.experimental.pallas import tpu as pltpu
from jax.sharding import PartitionSpec as P

MESH = pl.DeviceIdType.MESH
F, LEV, ROWS, CELLS, WIDE = 6, 32, 16, 360, 384
PARTS, LENGTH, KMAX, CAP = 8, 2880, 1024, 14
GROUPS, QUADS = LEV // 8, LEV // 8 * F
SLOT = QUADS
UNITS = CAP * SLOT
BLOCK = 6
SEGMENT = PARTS * BLOCK
HELP_SEGMENTS = ((0, 3), (1, 4))
OWN_SEGMENTS = (2, 5, 6)
BATCH = 8 * BLOCK
HALF = 1.0 / math.sqrt(2.0)


def tables():
    cells = np.arange(CELLS, dtype=np.int64)

    def angles(waves):
        return 2.0 * np.pi * ((cells[:, None] * waves[None, :]) % LENGTH) / LENGTH

    def halves(table):
        wide = np.asarray(table, np.float64)
        head = wide.astype(ml_dtypes.bfloat16)
        return head, (wide - head.astype(np.float64)).astype(ml_dtypes.bfloat16)

    pair = np.zeros((3, 2 * WIDE, 512))
    single = np.zeros((2, WIDE, 256))
    waves_pair = np.zeros((3, 1, 512), np.int32)
    waves_single = np.zeros((2, 1, 256), np.int32)
    for kind in (1, 2, 3):
        waves = kind + 8 * np.arange(-128, 128)
        cos, sin = np.cos(angles(waves)), np.sin(angles(waves))
        pair[kind - 1, :CELLS, :256] = cos
        pair[kind - 1, :CELLS, 256:] = -sin
        pair[kind - 1, WIDE : WIDE + CELLS, :256] = sin
        pair[kind - 1, WIDE : WIDE + CELLS, 256:] = cos
        waves_pair[kind - 1, 0] = np.concatenate([np.abs(waves)] * 2)
    for at, kind in enumerate((0, 4)):
        waves = kind + 8 * np.arange(128)
        single[at, :CELLS, :128] = np.cos(angles(waves))
        single[at, :CELLS, 128:] = -np.sin(angles(waves))
        waves_single[at, 0] = np.concatenate([waves] * 2)
    return (*halves(pair), *halves(single), waves_pair, waves_single)


def kernel(
    fields, inv_cos, c_lon, c_lat, polar_rows, bands, pair_hi, pair_lo, one_hi, one_lo, waves_pair, waves_one,
    pred, back,
    grid, lon_out, lon_in, slots, relay, pieces, result, spec, t_ph, t_pl, t_oh, t_ol, turned,
    tab_sem, lon_ss, lon_rs, lat_ss, lat_rs, help_ss, help_rs, own_ss, own_rs, self_sem, ret_ss, ret_rs, ret_self,
):
    t, i = lax.axis_index("lat"), lax.axis_index("lon")
    north, south = t < 2, t >= 14
    polar = north | south
    up = (t >= 2) & (t < 6)
    down = (t >= 10) & (t < 14)
    helper = up | down
    host = jnp.where(polar, t, jnp.where(up, lax.rem(t + 12, 16), lax.rem(t + 4, 16)))
    flip = host >= 14
    first = jnp.where(host < 2, host, jnp.where(flip, host - 12, 0)) * CAP

    loads = [
        pltpu.make_async_copy(src, dst, tab_sem.at[n])
        for n, (src, dst) in enumerate(((pair_hi, t_ph), (pair_lo, t_pl), (one_hi, t_oh), (one_lo, t_ol)))
    ]
    for load in loads:
        load.start()

    barrier = pltpu.get_barrier_semaphore()

    def greet(lat, lon):
        pl.semaphore_signal(barrier, inc=1, device_id=(lat, lon), device_id_type=MESH)

    for k in range(1, PARTS):
        greet(t, lax.rem(i + k, PARTS))

    @pl.when(t > 0)
    def _():
        greet(t - 1, i)

    @pl.when(t < 15)
    def _():
        greet(t + 1, i)

    @pl.when(polar)
    def _():
        for k in range(PARTS):
            greet(lax.rem(t + 4, 16), k)
            greet(lax.rem(t + 12, 16), k)

    @pl.when(helper)
    def _():
        for k in range(PARTS):
            greet(host, k)

    lane = lax.broadcasted_iota(jnp.int32, (8, 128), 1)

    def turn(at, _):
        g, pair = at // (F // 2), lax.rem(at, F // 2)
        low, high = [], []
        for odd in range(2):
            f = 2 * pair + odd
            base = pl.multiple_of(f * LEV * ROWS + g * 128, 128)
            turned[0, odd] = fields[pl.ds(base, 128), 0:128]
            turned[1, odd] = fields[pl.ds(base, 128), 128:256]
            turned[2, odd, :, 0 : CELLS - 256] = fields[pl.ds(base, 128), 256:CELLS]
            for r in range(ROWS):
                k = odd * 16 + r
                tiles = [turned[c, odd, pl.ds(r, 8, stride=ROWS), :] for c in range(3)]
                tiles[2] = jnp.where(lane < CELLS - 256, tiles[2], 0.0)
                for c in range(3):
                    grid[r + 3, g, f, :, 128 * c : 128 * (c + 1)] = tiles[c]
                mine = lane // 4 == k
                low.append(jnp.where(mine, pltpu.roll(tiles[0], 4 * k, axis=1), 0.0))
                high.append(jnp.where(mine, pltpu.roll(tiles[2], (4 * k + 128 - 101) % 128, axis=1), 0.0))
        lon_out[0, g, pair] = functools.reduce(jnp.add, low)
        lon_out[1, g, pair] = functools.reduce(jnp.add, high)
        return 0

    lax.fori_loop(0, GROUPS * F // 2, turn, 0)

    edge = jnp.where(t > 0, 1, 0) + jnp.where(t < 15, 1, 0)
    pl.semaphore_wait(barrier, PARTS - 1 + edge + jnp.where(polar, 2 * PARTS, 0) + jnp.where(helper, PARTS, 0))

    lon_copies = [
        pltpu.make_async_remote_copy(
            src_ref=lon_out.at[side], dst_ref=lon_in.at[side], send_sem=lon_ss.at[side], recv_sem=lon_rs.at[side],
            device_id=(t, lax.rem(i + shift, PARTS)), device_id_type=MESH,
        )
        for side, shift in ((0, PARTS - 1), (1, 1))
    ]
    for copy in lon_copies:
        copy.start()
    south_copy = pltpu.make_async_remote_copy(
        src_ref=grid.at[pl.ds(16, 3)], dst_ref=grid.at[pl.ds(0, 3)], send_sem=lat_ss.at[0], recv_sem=lat_rs.at[0],
        device_id=(jnp.minimum(t + 1, 15), i), device_id_type=MESH,
    )
    north_copy = pltpu.make_async_remote_copy(
        src_ref=grid.at[pl.ds(3, 3)], dst_ref=grid.at[pl.ds(19, 3)], send_sem=lat_ss.at[1], recv_sem=lat_rs.at[1],
        device_id=(jnp.maximum(t - 1, 0), i), device_id_type=MESH,
    )

    @pl.when(t < 15)
    def _():
        south_copy.start()

    @pl.when(t > 0)
    def _():
        north_copy.start()

    def clear(row0):
        def one(r, _):
            for g in range(GROUPS):
                for f in range(F):
                    grid[row0 + r, g, f] = jnp.zeros((8, WIDE), jnp.float32)
            return 0

        lax.fori_loop(0, 3, one, 0)

    @pl.when(t == 0)
    def _():
        clear(0)

    @pl.when(t == 15)
    def _():
        clear(19)

    for copy in lon_copies:
        copy.wait_recv()

    def wait_above():
        @pl.when(t > 0)
        def _():
            south_copy.wait_recv()

    def wait_below():
        @pl.when(t < 15)
        def _():
            north_copy.wait_recv()

    def others(act):
        def one(k, _):
            act(lax.rem(i + k, PARTS))
            return 0

        lax.fori_loop(1, PARTS, one, 0)

    def everyone(act):
        others(act)
        act(i)

    def units(segment, j):
        return pl.ds(segment * SEGMENT + j * BLOCK, BLOCK)

    def own_segment(block):
        return jnp.where(block == 0, OWN_SEGMENTS[0], OWN_SEGMENTS[1] - 1 + block)

    def help_send(which, block, j):
        return pltpu.make_async_remote_copy(
            src_ref=slots.at[units(HELP_SEGMENTS[which][block], j)], dst_ref=relay.at[block, j],
            send_sem=help_ss.at[which, block, j], recv_sem=help_rs.at[block, j],
            device_id=(lax.rem(t + (4, 12)[which], 16), i), device_id_type=MESH,
        )

    def own_send(block, p, j):
        return pltpu.make_async_remote_copy(
            src_ref=slots.at[units(own_segment(block), j)], dst_ref=pieces.at[block, p],
            send_sem=own_ss.at[block, j], recv_sem=own_rs.at[block, p],
            device_id=(t, j), device_id_type=MESH,
        )

    def own_local(block):
        return pltpu.make_async_copy(
            slots.at[units(own_segment(block), i)], pieces.at[block, i], self_sem.at[block]
        )

    def relay_send(block, p, j):
        return pltpu.make_async_remote_copy(
            src_ref=relay.at[block, j], dst_ref=pieces.at[block, p],
            send_sem=own_ss.at[block, j], recv_sem=own_rs.at[block, p],
            device_id=(t, j), device_id_type=MESH,
        )

    def relay_local(block):
        return pltpu.make_async_copy(relay.at[block, i], pieces.at[block, i], self_sem.at[block])

    def step(at, _):
        n, g = at // GROUPS, lax.rem(at, GROUPS)
        n = jnp.where(n < ROWS, n, jnp.where(n < ROWS + 3, n - ROWS, n - 6))
        r = jnp.where(flip, ROWS - 1 - n, n)
        scale = inv_cos[r] * (1.0 / 60.0)
        centre, along_lon, along_lat = [], [], []
        for f in range(F):
            k = (f % 2) * 16 + r
            east = pltpu.roll(lon_in[0, g, f // 2], lax.rem(104 + 128 - 4 * k, 128), axis=1)
            west = pltpu.roll(lon_in[1, g, f // 2], lax.rem(125 + 128 - 4 * k, 128), axis=1)
            mid = grid[r + 3, g, f]
            halo = jnp.where((lane >= 104) & (lane < 107), east, jnp.where(lane >= 125, west, 0.0))
            cells = jnp.concatenate([mid[:, :256], mid[:, 256:] + halo], axis=1)
            centre.append(mid)

            def at_cell(d):
                return pltpu.roll(cells, (WIDE - d) % WIDE, axis=1)

            along_lon.append(
                (45.0 * (at_cell(1) - at_cell(-1)) - 9.0 * (at_cell(2) - at_cell(-2)) + (at_cell(3) - at_cell(-3)))
                * scale
            )

            def at_row(d):
                return grid[r + 3 + d, g, f]

            along_lat.append(
                (45.0 * (at_row(1) - at_row(-1)) - 9.0 * (at_row(2) - at_row(-2)) + (at_row(3) - at_row(-3)))
                * (1.0 / 60.0)
            )
        for f in range(F):
            total = centre[f]
            for h in range(F):
                total = total + c_lon[f, h] * along_lon[h] + c_lat[f, h] * along_lat[h]
            pred[r, g * F + f] = jnp.where(lax.broadcasted_iota(jnp.int32, (8, WIDE), 1) < CELLS, total, 0.0)

        @pl.when(polar & (g == GROUPS - 1) & (n >= 2))
        def _():
            s = jnp.where(flip, CAP - 1 - (n - 2), n - 2)
            row = jnp.clip(polar_rows[first + s] - t * ROWS, 0, ROWS - 1)
            for q in range(SLOT):
                slots[(n - 2) * SLOT + q] = pred[row, q]

            for which in range(2):
                for block in range(2):

                    @pl.when(n == 2 * HELP_SEGMENTS[which][block] + 3)
                    def _():
                        everyone(lambda j: help_send(which, block, j).start())

            for block, segment in enumerate(OWN_SEGMENTS):

                @pl.when(n == 2 * segment + 3)
                def _():
                    others(lambda j: own_send(block, i, j).start())
                    own_local(block).start()

        return 0

    def rows_from(lo, hi):
        lax.fori_loop(lo * GROUPS, hi * GROUPS, step, 0)

    @pl.when(polar & jnp.logical_not(flip))
    def _():
        wait_above()

    @pl.when(polar & flip)
    def _():
        wait_below()

    rows_from(jnp.where(polar, 0, 3), 13)

    def ret_own(block, p, j):
        return pltpu.make_async_remote_copy(
            src_ref=result.at[block, p], dst_ref=back.at[units(own_segment(block), j)],
            send_sem=ret_ss.at[block, p], recv_sem=ret_rs.at[block, j],
            device_id=(t, p), device_id_type=MESH,
        )

    def ret_own_local(block):
        return pltpu.make_async_copy(
            result.at[block, i], back.at[units(own_segment(block), i)], ret_self.at[block]
        )

    def ret_help(which, block, p, j):
        return pltpu.make_async_remote_copy(
            src_ref=result.at[block, p], dst_ref=back.at[units(3 * block + which, j)],
            send_sem=ret_ss.at[block, p], recv_sem=ret_rs.at[3 + 2 * which + block, j],
            device_id=(host, p), device_id_type=MESH,
        )

    def matmul(wide, head, tail, back_again):
        top = wide.astype(jnp.bfloat16)
        low = (wide - top.astype(jnp.float32)).astype(jnp.bfloat16)
        dims = (((1,), (1 if back_again else 0,)), ((), ()))
        both = lax.dot_general(
            jnp.concatenate([top, low], axis=0), head, dims, preferred_element_type=jnp.float32
        )
        cross = lax.dot_general(top, tail, dims, preferred_element_type=jnp.float32)
        return both[:BATCH] + (both[BATCH:] + cross)

    def band_column(block):
        segment = jnp.where(polar, own_segment(block), 3 * block + jnp.where(up, 0, 1))
        start = segment * SEGMENT + i * BLOCK
        unit_of = lax.broadcasted_iota(jnp.int32, (BATCH, 1), 0) // 8
        column = jnp.zeros((BATCH, 1), jnp.int32)
        for n in range(BLOCK):
            s = jnp.minimum((start + n) // SLOT, CAP - 1)
            s = jnp.where(flip, CAP - 1 - s, s)
            column = jnp.where(unit_of == n, bands[first + s], column)
        return column

    def filter_block(block, _):
        @pl.when(polar)
        def _():
            others(lambda p: own_send(block, p, i).wait_recv())
            own_local(block).wait()

        @pl.when(helper)
        def _():
            others(lambda p: relay_send(block, p, i).wait_recv())
            relay_local(block).wait()

        def forward(n, _):
            x = [pieces[block, p, n] for p in range(PARTS)]
            e = [x[p] + x[p + 4] for p in range(4)]
            d = [x[p] - x[p + 4] for p in range(4)]
            here = pl.ds(pl.multiple_of(n * 8, 8), 8)
            minus, plus = HALF * (d[1] - d[3]), HALF * (d[1] + d[3])
            parts = (
                d[0] + minus, -plus - d[2],
                e[0] - e[2], e[3] - e[1],
                d[0] - minus, d[2] - plus,
                (e[0] + e[2]) + (e[1] + e[3]), (e[0] + e[2]) - (e[1] + e[3]),
            )
            for m, part in enumerate(parts):
                spec[here, m * WIDE : (m + 1) * WIDE] = part
            return 0

        lax.fori_loop(0, BLOCK, forward, 0)
        column = band_column(block)
        for m in range(3):
            here = slice(m * 2 * WIDE, (m + 1) * 2 * WIDE)
            waves = matmul(spec[:, here], t_ph[m], t_pl[m], False)
            waves = jnp.where(waves_pair[m] < column, waves * (2.0 / LENGTH), 0.0)
            spec[:, here] = matmul(waves, t_ph[m], t_pl[m], True)
        for m in range(2):
            here = slice((6 + m) * WIDE, (7 + m) * WIDE)
            waves = matmul(spec[:, here], t_oh[m], t_ol[m], False)
            factor = jnp.where(waves_one[m] == 0, 1.0 / LENGTH, 2.0 / LENGTH)
            waves = jnp.where(waves_one[m] < column, waves * factor, 0.0)
            spec[:, here] = matmul(waves, t_oh[m], t_ol[m], True)

        def inverse(n, _):
            here = pl.ds(pl.multiple_of(n * 8, 8), 8)
            r1, i1, r2, i2, r3, i3, z0, z4 = (spec[here, m * WIDE : (m + 1) * WIDE] for m in range(8))
            even, odd = z0 + z4, z0 - z4
            a, b = even + r2, even - r2
            c, d = odd - i2, odd + i2
            rr, ii = r1 + r3, i1 - i3
            u = HALF * ((r1 - r3) - (i1 + i3))
            v = HALF * ((r3 - r1) - (i1 + i3))
            outs = (a + rr, c + u, b - ii, d + v, a - rr, c - u, b + ii, d - v)
            for p, value in enumerate(outs):
                result[block, p, n] = value
            return 0

        lax.fori_loop(0, BLOCK, inverse, 0)

        @pl.when(polar)
        def _():
            others(lambda p: ret_own(block, p, i).start())
            ret_own_local(block).start()

        @pl.when(up)
        def _():
            everyone(lambda p: ret_help(0, block, p, i).start())

        @pl.when(down)
        def _():
            everyone(lambda p: ret_help(1, block, p, i).start())

        return 0

    def pass_on(block):
        @pl.when(helper)
        def _():
            def one(j):
                help_send(0, block, j).wait_recv()
                relay_send(block, i, j).start()

            others(one)
            help_send(0, block, i).wait_recv()
            relay_local(block).start()

    for load in loads:
        load.wait()
    pass_on(0)
    busy = jnp.where(polar | helper, 1, 0)
    lax.fori_loop(0, busy, filter_block, 0)
    pass_on(1)

    @pl.when(polar & jnp.logical_not(flip))
    def _():
        wait_below()

    @pl.when(polar & flip)
    def _():
        wait_above()

    @pl.when(jnp.logical_not(polar))
    def _():
        wait_above()
        wait_below()

    rows_from(ROWS + jnp.where(polar, 3, 0), ROWS + 6)
    lax.fori_loop(1, jnp.where(polar, 3, jnp.where(helper, 2, 1)), filter_block, 0)

    for copy in lon_copies:
        copy.wait_send()

    @pl.when(t < 15)
    def _():
        south_copy.wait_send()

    @pl.when(t > 0)
    def _():
        north_copy.wait_send()

    @pl.when(helper)
    def _():
        for block in range(2):
            others(lambda j: relay_send(block, i, j).wait_send())
            everyone(lambda p: ret_help(0, block, p, i).wait_send())

    @pl.when(polar)
    def _():
        for block in range(3):
            others(lambda j: own_send(block, i, j).wait_send())
            others(lambda p: ret_own(block, p, i).wait_send())
            others(lambda j: ret_own(block, i, j).wait_recv())
            ret_own_local(block).wait()
        for which in range(2):
            for block in range(2):
                everyone(lambda j: help_send(which, block, j).wait_send())
                everyone(lambda j: ret_help(which, block, i, j).wait_recv())


def place(polar_rows, pred, back, out, turned):
    t = lax.axis_index("lat")
    polar, flip = (t < 2) | (t >= 14), t >= 14
    first = jnp.where(t < 2, t, jnp.where(flip, t - 12, 0)) * CAP
    slot_of = []
    for r in range(ROWS):
        before, hit = 0, 0
        for s in range(CAP):
            row = polar_rows[first + s] - t * ROWS
            before = before + jnp.where(row < r, 1, 0)
            hit = hit + jnp.where(row == r, 1, 0)
        s = jnp.minimum(before, CAP - 1)
        slot_of.append((polar & (hit > 0), jnp.where(flip, CAP - 1 - s, s)))
    for odd in range(2):
        for r in range(ROWS):
            hit, s = slot_of[r]
            value = jnp.where(hit, back[s, 0, odd], pred[r, 0, odd])
            for c in range(3):
                turned[c, odd, pl.ds(r, 8, stride=ROWS), :] = value[:, 128 * c : 128 * (c + 1)]
        out[odd, 0, :, 0:128] = turned[0, odd]
        out[odd, 0, :, 128:256] = turned[1, odd]
        out[odd, 0, :, 256:CELLS] = turned[2, odd, :, 0 : CELLS - 256]


def local(fields, inv_cos, coupling_lon, coupling_lat, polar_rows, bands):
    smem, vmem, anywhere = (pl.BlockSpec(memory_space=space) for space in (pltpu.SMEM, pltpu.VMEM, pl.ANY))
    dma = pltpu.SemaphoreType.DMA
    pair_hi, pair_lo, one_hi, one_lo, waves_pair, waves_one = tables()
    f32, bf16 = jnp.float32, jnp.bfloat16
    pred, back = pl.pallas_call(
        kernel,
        out_shape=(
            jax.ShapeDtypeStruct((ROWS, QUADS, 8, WIDE), f32),
            jax.ShapeDtypeStruct((UNITS, 8, WIDE), f32),
        ),
        in_specs=[vmem] + [smem] * 5 + [anywhere] * 4 + [vmem] * 2,
        out_specs=(vmem, vmem),
        scratch_shapes=[
            pltpu.VMEM((ROWS + 6, GROUPS, F, 8, WIDE), f32),
            pltpu.VMEM((2, GROUPS, F // 2, 8, 128), f32),
            pltpu.VMEM((2, GROUPS, F // 2, 8, 128), f32),
            pltpu.VMEM((UNITS, 8, WIDE), f32),
            pltpu.VMEM((2, PARTS, BLOCK, 8, WIDE), f32),
            pltpu.VMEM((3, PARTS, BLOCK, 8, WIDE), f32),
            pltpu.VMEM((3, PARTS, BLOCK, 8, WIDE), f32),
            pltpu.VMEM((BATCH, 8 * WIDE), f32),
            pltpu.VMEM((3, 2 * WIDE, 512), bf16),
            pltpu.VMEM((3, 2 * WIDE, 512), bf16),
            pltpu.VMEM((2, WIDE, 256), bf16),
            pltpu.VMEM((2, WIDE, 256), bf16),
            pltpu.VMEM((3, 2, 128, 128), f32),
            dma((4,)),
            dma((2,)), dma((2,)), dma((2,)), dma((2,)),
            dma((2, 2, PARTS)), dma((2, PARTS)),
            dma((3, PARTS)), dma((3, PARTS)), dma((3,)),
            dma((3, PARTS)), dma((7, PARTS)), dma((3,)),
        ],
        compiler_params=pltpu.CompilerParams(
            collective_id=0, has_side_effects=True, vmem_limit_bytes=60 * 2**20
        ),
    )(
        fields.reshape(F * LEV * ROWS, CELLS),
        inv_cos,
        coupling_lon,
        coupling_lat,
        polar_rows,
        bands,
        jnp.asarray(pair_hi), jnp.asarray(pair_lo), jnp.asarray(one_hi), jnp.asarray(one_lo),
        jnp.asarray(waves_pair), jnp.asarray(waves_one),
    )
    out = pl.pallas_call(
        place,
        grid=(GROUPS, F // 2),
        out_shape=jax.ShapeDtypeStruct((F, GROUPS, 8 * ROWS, CELLS), f32),
        in_specs=[
            smem,
            pl.BlockSpec((ROWS, 1, 2, 8, WIDE), lambda g, pair: (0, g, pair, 0, 0)),
            pl.BlockSpec((CAP, 1, 2, 8, WIDE), lambda g, pair: (0, g, pair, 0, 0)),
        ],
        out_specs=pl.BlockSpec((2, 1, 8 * ROWS, CELLS), lambda g, pair: (pair, g, 0, 0)),
        scratch_shapes=[pltpu.VMEM((3, 2, 8 * ROWS, 128), f32)],
    )(
        polar_rows,
        pred.reshape(ROWS, GROUPS, F, 8, WIDE),
        back.reshape(CAP, GROUPS, F, 8, WIDE),
    )
    return out.reshape(F, LEV, ROWS, CELLS)


def solution(mesh):
    return jax.shard_map(
        local,
        mesh=mesh,
        in_specs=(P(None, None, "lat", "lon"), P("lat"), P(), P(), P(), P()),
        out_specs=P(None, None, "lat", "lon"),
        check_vma=False,
    )
```

```python
import functools
import math

import jax
import jax.numpy as jnp
import ml_dtypes
import numpy as np
from jax import lax
from jax.experimental import pallas as pl
from jax.experimental.pallas import tpu as pltpu
from jax.sharding import PartitionSpec as P

MESH = pl.DeviceIdType.MESH
F, LEV, ROWS, CELLS, WIDE = 6, 32, 16, 360, 384
PARTS, LENGTH, KMAX, CAP = 8, 2880, 1024, 14
GROUPS, QUADS = LEV // 8, LEV // 8 * F
SLOT = QUADS
UNITS = CAP * SLOT
BLOCK = 6
SEGMENT = PARTS * BLOCK
HELP_SEGMENTS = ((0, 3), (1, 4))
OWN_SEGMENTS = (2, 5, 6)
BATCH = 8 * BLOCK
HALF = 1.0 / math.sqrt(2.0)


def tables():
    cells = np.arange(CELLS, dtype=np.int64)

    def angles(waves):
        return 2.0 * np.pi * ((cells[:, None] * waves[None, :]) % LENGTH) / LENGTH

    def halves(table):
        wide = np.asarray(table, np.float64)
        head = wide.astype(ml_dtypes.bfloat16)
        return head, (wide - head.astype(np.float64)).astype(ml_dtypes.bfloat16)

    pair = np.zeros((3, 2 * WIDE, 512))
    single = np.zeros((2, WIDE, 256))
    waves_pair = np.zeros((3, 1, 512), np.int32)
    waves_single = np.zeros((2, 1, 256), np.int32)
    for kind in (1, 2, 3):
        waves = kind + 8 * np.arange(-128, 128)
        cos, sin = np.cos(angles(waves)), np.sin(angles(waves))
        pair[kind - 1, :CELLS, :256] = cos
        pair[kind - 1, :CELLS, 256:] = -sin
        pair[kind - 1, WIDE : WIDE + CELLS, :256] = sin
        pair[kind - 1, WIDE : WIDE + CELLS, 256:] = cos
        waves_pair[kind - 1, 0] = np.concatenate([np.abs(waves)] * 2)
    for at, kind in enumerate((0, 4)):
        waves = kind + 8 * np.arange(128)
        single[at, :CELLS, :128] = np.cos(angles(waves))
        single[at, :CELLS, 128:] = -np.sin(angles(waves))
        waves_single[at, 0] = np.concatenate([waves] * 2)
    return (*halves(pair), *halves(single), waves_pair, waves_single)


def kernel(
    fields, inv_cos, c_lon, c_lat, polar_rows, bands, pair_hi, pair_lo, one_hi, one_lo, waves_pair, waves_one,
    pred, back,
    grid, lon_out, lon_in, slots, relay, pieces, result, spec, t_ph, t_pl, t_oh, t_ol, turned,
    tab_sem, lon_ss, lon_rs, lat_ss, lat_rs, help_ss, help_rs, own_ss, own_rs, self_sem, ret_ss, ret_rs, ret_self,
):
    t, i = lax.axis_index("lat"), lax.axis_index("lon")
    north, south = t < 2, t >= 14
    polar = north | south
    up = (t >= 2) & (t < 6)
    down = (t >= 10) & (t < 14)
    helper = up | down
    host = jnp.where(polar, t, jnp.where(up, lax.rem(t + 12, 16), lax.rem(t + 4, 16)))
    flip = host >= 14
    first = jnp.where(host < 2, host, jnp.where(flip, host - 12, 0)) * CAP

    loads = [
        pltpu.make_async_copy(src, dst, tab_sem.at[n])
        for n, (src, dst) in enumerate(((pair_hi, t_ph), (pair_lo, t_pl), (one_hi, t_oh), (one_lo, t_ol)))
    ]
    for load in loads:
        load.start()

    barrier = pltpu.get_barrier_semaphore()

    def greet(lat, lon):
        pl.semaphore_signal(barrier, inc=1, device_id=(lat, lon), device_id_type=MESH)

    for k in range(1, PARTS):
        greet(t, lax.rem(i + k, PARTS))

    @pl.when(t > 0)
    def _():
        greet(t - 1, i)

    @pl.when(t < 15)
    def _():
        greet(t + 1, i)

    @pl.when(polar)
    def _():
        for k in range(PARTS):
            greet(lax.rem(t + 4, 16), k)
            greet(lax.rem(t + 12, 16), k)

    @pl.when(helper)
    def _():
        for k in range(PARTS):
            greet(host, k)

    lane = lax.broadcasted_iota(jnp.int32, (8, 128), 1)

    def turn(at, _):
        g, pair = at // (F // 2), lax.rem(at, F // 2)
        low, high = [], []
        for odd in range(2):
            f = 2 * pair + odd
            base = pl.multiple_of(f * LEV * ROWS + g * 128, 128)
            turned[0, odd] = fields[pl.ds(base, 128), 0:128]
            turned[1, odd] = fields[pl.ds(base, 128), 128:256]
            turned[2, odd, :, 0 : CELLS - 256] = fields[pl.ds(base, 128), 256:CELLS]
            for r in range(ROWS):
                k = odd * 16 + r
                tiles = [turned[c, odd, pl.ds(r, 8, stride=ROWS), :] for c in range(3)]
                tiles[2] = jnp.where(lane < CELLS - 256, tiles[2], 0.0)
                for c in range(3):
                    grid[r + 3, g, f, :, 128 * c : 128 * (c + 1)] = tiles[c]
                mine = lane // 4 == k
                low.append(jnp.where(mine, pltpu.roll(tiles[0], 4 * k, axis=1), 0.0))
                high.append(jnp.where(mine, pltpu.roll(tiles[2], (4 * k + 128 - 101) % 128, axis=1), 0.0))
        lon_out[0, g, pair] = functools.reduce(jnp.add, low)
        lon_out[1, g, pair] = functools.reduce(jnp.add, high)
        return 0

    lax.fori_loop(0, GROUPS * F // 2, turn, 0)

    edge = jnp.where(t > 0, 1, 0) + jnp.where(t < 15, 1, 0)
    pl.semaphore_wait(barrier, PARTS - 1 + edge + jnp.where(polar, 2 * PARTS, 0) + jnp.where(helper, PARTS, 0))

    lon_copies = [
        pltpu.make_async_remote_copy(
            src_ref=lon_out.at[side], dst_ref=lon_in.at[side], send_sem=lon_ss.at[side], recv_sem=lon_rs.at[side],
            device_id=(t, lax.rem(i + shift, PARTS)), device_id_type=MESH,
        )
        for side, shift in ((0, PARTS - 1), (1, 1))
    ]
    for copy in lon_copies:
        copy.start()
    south_copy = pltpu.make_async_remote_copy(
        src_ref=grid.at[pl.ds(16, 3)], dst_ref=grid.at[pl.ds(0, 3)], send_sem=lat_ss.at[0], recv_sem=lat_rs.at[0],
        device_id=(jnp.minimum(t + 1, 15), i), device_id_type=MESH,
    )
    north_copy = pltpu.make_async_remote_copy(
        src_ref=grid.at[pl.ds(3, 3)], dst_ref=grid.at[pl.ds(19, 3)], send_sem=lat_ss.at[1], recv_sem=lat_rs.at[1],
        device_id=(jnp.maximum(t - 1, 0), i), device_id_type=MESH,
    )

    @pl.when(t < 15)
    def _():
        south_copy.start()

    @pl.when(t > 0)
    def _():
        north_copy.start()

    def clear(row0):
        def one(r, _):
            for g in range(GROUPS):
                for f in range(F):
                    grid[row0 + r, g, f] = jnp.zeros((8, WIDE), jnp.float32)
            return 0

        lax.fori_loop(0, 3, one, 0)

    @pl.when(t == 0)
    def _():
        clear(0)

    @pl.when(t == 15)
    def _():
        clear(19)

    for copy in lon_copies:
        copy.wait_recv()

    def wait_above():
        @pl.when(t > 0)
        def _():
            south_copy.wait_recv()

    def wait_below():
        @pl.when(t < 15)
        def _():
            north_copy.wait_recv()

    def others(act):
        def one(k, _):
            act(lax.rem(i + k, PARTS))
            return 0

        lax.fori_loop(1, PARTS, one, 0)

    def everyone(act):
        others(act)
        act(i)

    def units(segment, j):
        return pl.ds(segment * SEGMENT + j * BLOCK, BLOCK)

    def own_segment(block):
        return jnp.where(block == 0, OWN_SEGMENTS[0], OWN_SEGMENTS[1] - 1 + block)

    def help_send(which, block, j):
        return pltpu.make_async_remote_copy(
            src_ref=slots.at[units(HELP_SEGMENTS[which][block], j)], dst_ref=relay.at[block, j],
            send_sem=help_ss.at[which, block, j], recv_sem=help_rs.at[block, j],
            device_id=(lax.rem(t + (4, 12)[which], 16), i), device_id_type=MESH,
        )

    def own_send(block, p, j):
        return pltpu.make_async_remote_copy(
            src_ref=slots.at[units(own_segment(block), j)], dst_ref=pieces.at[block, p],
            send_sem=own_ss.at[block, j], recv_sem=own_rs.at[block, p],
            device_id=(t, j), device_id_type=MESH,
        )

    def own_local(block):
        return pltpu.make_async_copy(
            slots.at[units(own_segment(block), i)], pieces.at[block, i], self_sem.at[block]
        )

    def relay_send(block, p, j):
        return pltpu.make_async_remote_copy(
            src_ref=relay.at[block, j], dst_ref=pieces.at[block, p],
            send_sem=own_ss.at[block, j], recv_sem=own_rs.at[block, p],
            device_id=(t, j), device_id_type=MESH,
        )

    def relay_local(block):
        return pltpu.make_async_copy(relay.at[block, i], pieces.at[block, i], self_sem.at[block])

    def step(at, _):
        n, g = at // GROUPS, lax.rem(at, GROUPS)
        n = jnp.where(n < ROWS, n, jnp.where(n < ROWS + 3, n - ROWS, n - 6))
        r = jnp.where(flip, ROWS - 1 - n, n)
        scale = inv_cos[r] * (1.0 / 60.0)
        centre, along_lon, along_lat = [], [], []
        for f in range(F):
            k = (f % 2) * 16 + r
            east = pltpu.roll(lon_in[0, g, f // 2], lax.rem(104 + 128 - 4 * k, 128), axis=1)
            west = pltpu.roll(lon_in[1, g, f // 2], lax.rem(125 + 128 - 4 * k, 128), axis=1)
            mid = grid[r + 3, g, f]
            halo = jnp.where((lane >= 104) & (lane < 107), east, jnp.where(lane >= 125, west, 0.0))
            cells = jnp.concatenate([mid[:, :256], mid[:, 256:] + halo], axis=1)
            centre.append(mid)

            def at_cell(d):
                return pltpu.roll(cells, (WIDE - d) % WIDE, axis=1)

            along_lon.append(
                (45.0 * (at_cell(1) - at_cell(-1)) - 9.0 * (at_cell(2) - at_cell(-2)) + (at_cell(3) - at_cell(-3)))
                * scale
            )

            def at_row(d):
                return grid[r + 3 + d, g, f]

            along_lat.append(
                (45.0 * (at_row(1) - at_row(-1)) - 9.0 * (at_row(2) - at_row(-2)) + (at_row(3) - at_row(-3)))
                * (1.0 / 60.0)
            )
        for f in range(F):
            total = centre[f]
            for h in range(F):
                total = total + c_lon[f, h] * along_lon[h] + c_lat[f, h] * along_lat[h]
            pred[r, g * F + f] = jnp.where(lax.broadcasted_iota(jnp.int32, (8, WIDE), 1) < CELLS, total, 0.0)

        @pl.when(polar & (g == GROUPS - 1) & (n >= 2))
        def _():
            s = jnp.where(flip, CAP - 1 - (n - 2), n - 2)
            row = jnp.clip(polar_rows[first + s] - t * ROWS, 0, ROWS - 1)
            for q in range(SLOT):
                slots[(n - 2) * SLOT + q] = pred[row, q]

            for which in range(2):
                for block in range(2):

                    @pl.when(n == 2 * HELP_SEGMENTS[which][block] + 3)
                    def _():
                        everyone(lambda j: help_send(which, block, j).start())

            for block, segment in enumerate(OWN_SEGMENTS):

                @pl.when(n == 2 * segment + 3)
                def _():
                    others(lambda j: own_send(block, i, j).start())
                    own_local(block).start()

        return 0

    def rows_from(lo, hi):
        lax.fori_loop(lo * GROUPS, hi * GROUPS, step, 0)

    @pl.when(polar & jnp.logical_not(flip))
    def _():
        wait_above()

    @pl.when(polar & flip)
    def _():
        wait_below()

    rows_from(jnp.where(polar, 0, 3), 13)

    def ret_own(block, p, j):
        return pltpu.make_async_remote_copy(
            src_ref=result.at[block, p], dst_ref=back.at[units(own_segment(block), j)],
            send_sem=ret_ss.at[block, p], recv_sem=ret_rs.at[block, j],
            device_id=(t, p), device_id_type=MESH,
        )

    def ret_own_local(block):
        return pltpu.make_async_copy(
            result.at[block, i], back.at[units(own_segment(block), i)], ret_self.at[block]
        )

    def ret_help(which, block, p, j):
        return pltpu.make_async_remote_copy(
            src_ref=result.at[block, p], dst_ref=back.at[units(3 * block + which, j)],
            send_sem=ret_ss.at[block, p], recv_sem=ret_rs.at[3 + 2 * which + block, j],
            device_id=(host, p), device_id_type=MESH,
        )

    def matmul(wide, head, tail, back_again):
        top = wide.astype(jnp.bfloat16)
        low = (wide - top.astype(jnp.float32)).astype(jnp.bfloat16)
        dims = (((1,), (1 if back_again else 0,)), ((), ()))
        both = lax.dot_general(
            jnp.concatenate([top, low], axis=0), head, dims, preferred_element_type=jnp.float32
        )
        cross = lax.dot_general(top, tail, dims, preferred_element_type=jnp.float32)
        return both[:BATCH] + (both[BATCH:] + cross)

    def band_column(block):
        segment = jnp.where(polar, own_segment(block), 3 * block + jnp.where(up, 0, 1))
        start = segment * SEGMENT + i * BLOCK
        unit_of = lax.broadcasted_iota(jnp.int32, (BATCH, 1), 0) // 8
        column = jnp.zeros((BATCH, 1), jnp.int32)
        for n in range(BLOCK):
            s = jnp.minimum((start + n) // SLOT, CAP - 1)
            s = jnp.where(flip, CAP - 1 - s, s)
            column = jnp.where(unit_of == n, bands[first + s], column)
        return column

    def filter_block(block, _):
        @pl.when(polar)
        def _():
            others(lambda p: own_send(block, p, i).wait_recv())
            own_local(block).wait()

        @pl.when(helper)
        def _():
            others(lambda p: relay_send(block, p, i).wait_recv())
            relay_local(block).wait()

        def forward(n, _):
            x = [pieces[block, p, n] for p in range(PARTS)]
            e = [x[p] + x[p + 4] for p in range(4)]
            d = [x[p] - x[p + 4] for p in range(4)]
            here = pl.ds(pl.multiple_of(n * 8, 8), 8)
            minus, plus = HALF * (d[1] - d[3]), HALF * (d[1] + d[3])
            parts = (
                d[0] + minus, -plus - d[2],
                e[0] - e[2], e[3] - e[1],
                d[0] - minus, d[2] - plus,
                (e[0] + e[2]) + (e[1] + e[3]), (e[0] + e[2]) - (e[1] + e[3]),
            )
            for m, part in enumerate(parts):
                spec[here, m * WIDE : (m + 1) * WIDE] = part
            return 0

        lax.fori_loop(0, BLOCK, forward, 0)
        column = band_column(block)
        for m in range(3):
            here = slice(m * 2 * WIDE, (m + 1) * 2 * WIDE)
            waves = matmul(spec[:, here], t_ph[m], t_pl[m], False)
            waves = jnp.where(waves_pair[m] < column, waves * (2.0 / LENGTH), 0.0)
            spec[:, here] = matmul(waves, t_ph[m], t_pl[m], True)
        for m in range(2):
            here = slice((6 + m) * WIDE, (7 + m) * WIDE)
            waves = matmul(spec[:, here], t_oh[m], t_ol[m], False)
            factor = jnp.where(waves_one[m] == 0, 1.0 / LENGTH, 2.0 / LENGTH)
            waves = jnp.where(waves_one[m] < column, waves * factor, 0.0)
            spec[:, here] = matmul(waves, t_oh[m], t_ol[m], True)

        def inverse(n, _):
            here = pl.ds(pl.multiple_of(n * 8, 8), 8)
            r1, i1, r2, i2, r3, i3, z0, z4 = (spec[here, m * WIDE : (m + 1) * WIDE] for m in range(8))
            even, odd = z0 + z4, z0 - z4
            a, b = even + r2, even - r2
            c, d = odd - i2, odd + i2
            rr, ii = r1 + r3, i1 - i3
            u = HALF * ((r1 - r3) - (i1 + i3))
            v = HALF * ((r3 - r1) - (i1 + i3))
            outs = (a + rr, c + u, b - ii, d + v, a - rr, c - u, b + ii, d - v)
            for p, value in enumerate(outs):
                result[block, p, n] = value
            return 0

        lax.fori_loop(0, BLOCK, inverse, 0)

        @pl.when(polar)
        def _():
            others(lambda p: ret_own(block, p, i).start())
            ret_own_local(block).start()

        @pl.when(up)
        def _():
            everyone(lambda p: ret_help(0, block, p, i).start())

        @pl.when(down)
        def _():
            everyone(lambda p: ret_help(1, block, p, i).start())

        return 0

    def pass_on(block):
        @pl.when(helper)
        def _():
            def one(j):
                help_send(0, block, j).wait_recv()
                relay_send(block, i, j).start()

            others(one)
            help_send(0, block, i).wait_recv()
            relay_local(block).start()

    for load in loads:
        load.wait()
    pass_on(0)
    busy = jnp.where(polar | helper, 1, 0)
    lax.fori_loop(0, busy, filter_block, 0)
    pass_on(1)

    @pl.when(polar & jnp.logical_not(flip))
    def _():
        wait_below()

    @pl.when(polar & flip)
    def _():
        wait_above()

    @pl.when(jnp.logical_not(polar))
    def _():
        wait_above()
        wait_below()

    rows_from(ROWS + jnp.where(polar, 3, 0), ROWS + 6)
    lax.fori_loop(1, jnp.where(polar, 3, jnp.where(helper, 2, 1)), filter_block, 0)

    for copy in lon_copies:
        copy.wait_send()

    @pl.when(t < 15)
    def _():
        south_copy.wait_send()

    @pl.when(t > 0)
    def _():
        north_copy.wait_send()

    @pl.when(helper)
    def _():
        for block in range(2):
            others(lambda j: relay_send(block, i, j).wait_send())
            everyone(lambda p: ret_help(0, block, p, i).wait_send())

    @pl.when(polar)
    def _():
        for block in range(3):
            others(lambda j: own_send(block, i, j).wait_send())
            others(lambda p: ret_own(block, p, i).wait_send())
            others(lambda j: ret_own(block, i, j).wait_recv())
            ret_own_local(block).wait()
        for which in range(2):
            for block in range(2):
                everyone(lambda j: help_send(which, block, j).wait_send())
                everyone(lambda j: ret_help(which, block, i, j).wait_recv())


def place(polar_rows, pred, back, out, turned, ready, sems):
    t = lax.axis_index("lat")
    polar, flip = (t < 2) | (t >= 14), t >= 14
    first = jnp.where(t < 2, t, jnp.where(flip, t - 12, 0)) * CAP
    slot_of = []
    for r in range(ROWS):
        before, hit = 0, 0
        for s in range(CAP):
            row = polar_rows[first + s] - t * ROWS
            before = before + jnp.where(row < r, 1, 0)
            hit = hit + jnp.where(row == r, 1, 0)
        s = jnp.minimum(before, CAP - 1)
        slot_of.append((polar & (hit > 0), jnp.where(flip, CAP - 1 - s, s)))

    def leave(at):
        return pltpu.make_async_copy(ready.at[at], out.at[at], sems.at[at])

    def one(at, _):
        f, g = at // GROUPS, lax.rem(at, GROUPS)
        q = g * F + f
        for r in range(ROWS):
            hit, s = slot_of[r]
            value = jnp.where(hit, back[s * SLOT + q], pred[r, q])
            for c in range(3):
                turned[c, pl.ds(r, 8, stride=ROWS), :] = value[:, 128 * c : 128 * (c + 1)]
        ready[at, :, 0:128] = turned[0]
        ready[at, :, 128:256] = turned[1]
        ready[at, :, 256:CELLS] = turned[2, :, 0 : CELLS - 256]
        leave(at).start()
        return 0

    lax.fori_loop(0, QUADS, one, 0)

    def left(at, _):
        leave(at).wait()
        return 0

    lax.fori_loop(0, QUADS, left, 0)


def local(fields, inv_cos, coupling_lon, coupling_lat, polar_rows, bands):
    stay = functools.partial(pltpu.with_memory_space_constraint, memory_space=pltpu.HBM)
    smem, vmem, anywhere = (pl.BlockSpec(memory_space=space) for space in (pltpu.SMEM, pltpu.VMEM, pl.ANY))
    dma = pltpu.SemaphoreType.DMA
    pair_hi, pair_lo, one_hi, one_lo, waves_pair, waves_one = tables()
    f32, bf16 = jnp.float32, jnp.bfloat16
    pred, back = pl.pallas_call(
        kernel,
        out_shape=(
            pltpu.VMEM((ROWS, QUADS, 8, WIDE), f32),
            pltpu.VMEM((UNITS, 8, WIDE), f32),
        ),
        in_specs=[vmem] + [smem] * 5 + [anywhere] * 4 + [vmem] * 2,
        out_specs=(vmem, vmem),
        scratch_shapes=[
            pltpu.VMEM((ROWS + 6, GROUPS, F, 8, WIDE), f32),
            pltpu.VMEM((2, GROUPS, F // 2, 8, 128), f32),
            pltpu.VMEM((2, GROUPS, F // 2, 8, 128), f32),
            pltpu.VMEM((UNITS, 8, WIDE), f32),
            pltpu.VMEM((2, PARTS, BLOCK, 8, WIDE), f32),
            pltpu.VMEM((3, PARTS, BLOCK, 8, WIDE), f32),
            pltpu.VMEM((3, PARTS, BLOCK, 8, WIDE), f32),
            pltpu.VMEM((BATCH, 8 * WIDE), f32),
            pltpu.VMEM((3, 2 * WIDE, 512), bf16),
            pltpu.VMEM((3, 2 * WIDE, 512), bf16),
            pltpu.VMEM((2, WIDE, 256), bf16),
            pltpu.VMEM((2, WIDE, 256), bf16),
            pltpu.VMEM((3, 2, 128, 128), f32),
            dma((4,)),
            dma((2,)), dma((2,)), dma((2,)), dma((2,)),
            dma((2, 2, PARTS)), dma((2, PARTS)),
            dma((3, PARTS)), dma((3, PARTS)), dma((3,)),
            dma((3, PARTS)), dma((7, PARTS)), dma((3,)),
        ],
        compiler_params=pltpu.CompilerParams(
            collective_id=0, has_side_effects=True, vmem_limit_bytes=40 * 2**20
        ),
    )(
        stay(fields.reshape(F * LEV * ROWS, CELLS)),
        *(stay(x) for x in (inv_cos, coupling_lon, coupling_lat, polar_rows, bands)),
        *(stay(jnp.asarray(x)) for x in (pair_hi, pair_lo, one_hi, one_lo, waves_pair, waves_one)),
    )
    out = pl.pallas_call(
        place,
        out_shape=jax.ShapeDtypeStruct((QUADS, 8 * ROWS, CELLS), f32),
        in_specs=[smem, vmem, vmem],
        out_specs=anywhere,
        scratch_shapes=[
            pltpu.VMEM((3, 8 * ROWS, 128), f32),
            pltpu.VMEM((QUADS, 8 * ROWS, CELLS), f32),
            dma((QUADS,)),
        ],
        compiler_params=pltpu.CompilerParams(vmem_limit_bytes=24 * 2**20),
    )(stay(polar_rows), pred, back)
    return out.reshape(F, LEV, ROWS, CELLS)


def solution(mesh):
    return jax.shard_map(
        local,
        mesh=mesh,
        in_specs=(P(None, None, "lat", "lon"), P("lat"), P(), P(), P(), P()),
        out_specs=P(None, None, "lat", "lon"),
        check_vma=False,
    )
```

```python
import functools
import math

import jax
import jax.numpy as jnp
import ml_dtypes
import numpy as np
from jax import lax
from jax.experimental import pallas as pl
from jax.experimental.pallas import tpu as pltpu
from jax.sharding import PartitionSpec as P

MESH = pl.DeviceIdType.MESH
F, LEV, ROWS, CELLS, WIDE = 6, 32, 16, 360, 384
PARTS, LENGTH, KMAX, CAP = 8, 2880, 1024, 14
GROUPS, QUADS = LEV // 8, LEV // 8 * F
SLOT = QUADS
UNITS = CAP * SLOT
BLOCK = 3
SEGMENT = PARTS * BLOCK
HELP_SEGMENTS = ((0, 3, 6, 9, 12), (1, 4, 7, 10))
OWN_SEGMENTS = (2, 5, 8, 11, 13)
MOST = 5
ROOM = 4
BATCH = 8 * ROOM
HALF = 1.0 / math.sqrt(2.0)


def tables():
    cells = np.arange(CELLS, dtype=np.int64)

    def angles(waves):
        return 2.0 * np.pi * ((cells[:, None] * waves[None, :]) % LENGTH) / LENGTH

    def halves(table):
        wide = np.asarray(table, np.float64)
        head = wide.astype(ml_dtypes.bfloat16)
        return head, (wide - head.astype(np.float64)).astype(ml_dtypes.bfloat16)

    pair = np.zeros((3, 2 * WIDE, 512))
    single = np.zeros((2, WIDE, 256))
    waves_pair = np.zeros((3, 1, 512), np.int32)
    waves_single = np.zeros((2, 1, 256), np.int32)
    for kind in (1, 2, 3):
        waves = kind + 8 * np.arange(-128, 128)
        cos, sin = np.cos(angles(waves)), np.sin(angles(waves))
        pair[kind - 1, :CELLS, :256] = cos
        pair[kind - 1, :CELLS, 256:] = -sin
        pair[kind - 1, WIDE : WIDE + CELLS, :256] = sin
        pair[kind - 1, WIDE : WIDE + CELLS, 256:] = cos
        waves_pair[kind - 1, 0] = np.concatenate([np.abs(waves)] * 2)
    for at, kind in enumerate((0, 4)):
        waves = kind + 8 * np.arange(128)
        single[at, :CELLS, :128] = np.cos(angles(waves))
        single[at, :CELLS, 128:] = -np.sin(angles(waves))
        waves_single[at, 0] = np.concatenate([waves] * 2)
    gaps = np.zeros((WIDE, WIDE))
    for d, factor in ((1, 45.0), (2, -9.0), (3, 1.0)):
        gaps += factor * (np.roll(np.eye(WIDE), d, axis=0) - np.roll(np.eye(WIDE), -d, axis=0))
    return (*halves(pair), *halves(single), waves_pair, waves_single, gaps.astype(ml_dtypes.bfloat16))


def kernel(
    fields, inv_cos, c_lon, c_lat, polar_rows, bands, pair_hi, pair_lo, one_hi, one_lo, waves_pair, waves_one, gap_table,
    pred, back,
    grid, lon_out, lon_in, slots, relay, pieces, result, spec, t_ph, t_pl, t_oh, t_ol, turned, row, along,
    tab_sem, lon_ss, lon_rs, lat_ss, lat_rs, slot_ss, help_rs, own_rs, ret_ss, ret_rs,
):
    t, i = lax.axis_index("lat"), lax.axis_index("lon")
    north, south = t < 2, t >= 14
    polar = north | south
    up = ((t >= 2) & (t < 4)) | ((t >= 12) & (t < 14))
    down = ((t >= 4) & (t < 6)) | ((t >= 10) & (t < 12))
    helper = up | down
    host = jnp.where(polar, t, lax.rem(t + jnp.where(t < 6, 12, 4), 16))
    flip = host >= 14
    first = jnp.where(host < 2, host, jnp.where(flip, host - 12, 0)) * CAP

    loads = [
        pltpu.make_async_copy(src, dst, tab_sem.at[n])
        for n, (src, dst) in enumerate(((pair_hi, t_ph), (pair_lo, t_pl), (one_hi, t_oh), (one_lo, t_ol)))
    ]
    for load in loads:
        load.start()

    barrier = pltpu.get_barrier_semaphore()

    def greet(lat, lon):
        pl.semaphore_signal(barrier, inc=1, device_id=(lat, lon), device_id_type=MESH)

    for k in range(1, PARTS):
        greet(t, lax.rem(i + k, PARTS))

    @pl.when(t > 0)
    def _():
        greet(t - 1, i)

    @pl.when(t < 15)
    def _():
        greet(t + 1, i)

    @pl.when(polar)
    def _():
        for k in range(PARTS):
            greet(lax.rem(t + 4, 16), k)
            greet(lax.rem(t + 12, 16), k)

    @pl.when(helper)
    def _():
        for k in range(PARTS):
            greet(host, k)

    lane = lax.broadcasted_iota(jnp.int32, (8, 128), 1)

    def turn(at, _):
        g, pair = at // (F // 2), lax.rem(at, F // 2)
        low, high = [], []
        for odd in range(2):
            f = 2 * pair + odd
            base = pl.multiple_of(f * LEV * ROWS + g * 128, 128)
            turned[0, odd] = fields[pl.ds(base, 128), 0:128]
            turned[1, odd] = fields[pl.ds(base, 128), 128:256]
            turned[2, odd, :, 0 : CELLS - 256] = fields[pl.ds(base, 128), 256:CELLS]
            for r in range(ROWS):
                k = odd * 16 + r
                tiles = [turned[c, odd, pl.ds(r, 8, stride=ROWS), :] for c in range(3)]
                tiles[2] = jnp.where(lane < CELLS - 256, tiles[2], 0.0)
                for c in range(3):
                    grid[r + 3, g, f, :, 128 * c : 128 * (c + 1)] = tiles[c]
                mine = lane // 4 == k
                low.append(jnp.where(mine, pltpu.roll(tiles[0], 4 * k, axis=1), 0.0))
                high.append(jnp.where(mine, pltpu.roll(tiles[2], (4 * k + 128 - 101) % 128, axis=1), 0.0))
        lon_out[0, g, pair] = functools.reduce(jnp.add, low)
        lon_out[1, g, pair] = functools.reduce(jnp.add, high)
        return 0

    lax.fori_loop(0, GROUPS * F // 2, turn, 0)

    edge = jnp.where(t > 0, 1, 0) + jnp.where(t < 15, 1, 0)
    pl.semaphore_wait(barrier, PARTS - 1 + edge + jnp.where(polar, 2 * PARTS, 0) + jnp.where(helper, PARTS, 0))

    lon_copies = [
        pltpu.make_async_remote_copy(
            src_ref=lon_out.at[side], dst_ref=lon_in.at[side], send_sem=lon_ss.at[side], recv_sem=lon_rs.at[side],
            device_id=(t, lax.rem(i + shift, PARTS)), device_id_type=MESH,
        )
        for side, shift in ((0, PARTS - 1), (1, 1))
    ]
    for copy in lon_copies:
        copy.start()
    south_copy = pltpu.make_async_remote_copy(
        src_ref=grid.at[pl.ds(16, 3)], dst_ref=grid.at[pl.ds(0, 3)], send_sem=lat_ss.at[0], recv_sem=lat_rs.at[0],
        device_id=(jnp.minimum(t + 1, 15), i), device_id_type=MESH,
    )
    north_copy = pltpu.make_async_remote_copy(
        src_ref=grid.at[pl.ds(3, 3)], dst_ref=grid.at[pl.ds(19, 3)], send_sem=lat_ss.at[1], recv_sem=lat_rs.at[1],
        device_id=(jnp.maximum(t - 1, 0), i), device_id_type=MESH,
    )

    @pl.when(t < 15)
    def _():
        south_copy.start()

    @pl.when(t > 0)
    def _():
        north_copy.start()

    def clear(row0):
        def one(r, _):
            for g in range(GROUPS):
                for f in range(F):
                    grid[row0 + r, g, f] = jnp.zeros((8, WIDE), jnp.float32)
            return 0

        lax.fori_loop(0, 3, one, 0)

    @pl.when(t == 0)
    def _():
        clear(0)

    @pl.when(t == 15)
    def _():
        clear(19)

    for copy in lon_copies:
        copy.wait_recv()

    def wait_above():
        @pl.when(t > 0)
        def _():
            south_copy.wait_recv()

    def wait_below():
        @pl.when(t < 15)
        def _():
            north_copy.wait_recv()

    def others(act):
        def one(k, _):
            act(lax.rem(i + k, PARTS))
            return 0

        lax.fori_loop(1, PARTS, one, 0)

    def everyone(act):
        others(act)
        act(i)

    def await_bytes(ref, sem):
        pltpu.make_async_copy(ref, ref, sem).wait()

    def units(segment, j):
        return pl.ds(segment * SEGMENT + j * BLOCK, BLOCK)

    def own_segment(block):
        return 2 + 3 * block - block // 4

    def help_send(which, block, j):
        return pltpu.make_async_remote_copy(
            src_ref=slots.at[units(3 * block + which, j)], dst_ref=relay.at[block, j],
            send_sem=slot_ss, recv_sem=help_rs.at[block],
            device_id=(lax.rem(t + jnp.where(flip, (4, 12)[which], (12, 4)[which]), 16), i), device_id_type=MESH,
        )

    def own_send(block, p, j):
        return pltpu.make_async_remote_copy(
            src_ref=slots.at[units(own_segment(block), j)], dst_ref=pieces.at[block, p],
            send_sem=slot_ss, recv_sem=own_rs.at[block],
            device_id=(t, j), device_id_type=MESH,
        )

    def own_local(block):
        return pltpu.make_async_copy(
            slots.at[units(own_segment(block), i)], pieces.at[block, i], own_rs.at[block]
        )

    def relay_send(block, p, j):
        return pltpu.make_async_remote_copy(
            src_ref=relay.at[block, j], dst_ref=pieces.at[block, p],
            send_sem=slot_ss, recv_sem=own_rs.at[block],
            device_id=(t, j), device_id_type=MESH,
        )

    def relay_local(block):
        return pltpu.make_async_copy(relay.at[block, i], pieces.at[block, i], own_rs.at[block])

    def step(at, _):
        n = jnp.where(at < ROWS, at, jnp.where(at < ROWS + 3, at - ROWS, at - 6))
        r = jnp.where(flip, ROWS - 1 - n, n)
        scale = inv_cos[r] * (1.0 / 60.0)
        for g in range(GROUPS):
            for f in range(F):
                k = (f % 2) * 16 + r
                east = pltpu.roll(lon_in[0, g, f // 2], lax.rem(104 + 128 - 4 * k, 128), axis=1)
                west = pltpu.roll(lon_in[1, g, f // 2], lax.rem(125 + 128 - 4 * k, 128), axis=1)
                halo = jnp.where((lane >= 104) & (lane < 107), east, jnp.where(lane >= 125, west, 0.0))
                here = slice((g * F + f) * 8, (g * F + f + 1) * 8)
                row[here, 0:256] = grid[r + 3, g, f, :, 0:256]
                row[here, 256:WIDE] = grid[r + 3, g, f, :, 256:WIDE] + halo
        top = row[...].astype(jnp.bfloat16)
        low = (row[...] - top.astype(jnp.float32)).astype(jnp.bfloat16)
        both = jnp.dot(
            jnp.concatenate([top, low], axis=0), gap_table[...], preferred_element_type=jnp.float32
        )
        along[...] = (both[: QUADS * 8] + both[QUADS * 8 :]) * scale

        for g in range(GROUPS):
            along_lat, along_lon = [], []
            for f in range(F):

                def at_row(d):
                    return grid[r + 3 + d, g, f]

                along_lat.append(
                    (45.0 * (at_row(1) - at_row(-1)) - 9.0 * (at_row(2) - at_row(-2)) + (at_row(3) - at_row(-3)))
                    * (1.0 / 60.0)
                )
                along_lon.append(along[(g * F + f) * 8 : (g * F + f + 1) * 8, :])
            for f in range(F):
                total = grid[r + 3, g, f]
                for h in range(F):
                    total = total + c_lon[f, h] * along_lon[h] + c_lat[f, h] * along_lat[h]
                pred[r, g * F + f, :, 0:256] = total[:, 0:256]
                pred[r, g * F + f, :, 256:WIDE] = jnp.where(lane < CELLS - 256, total[:, 256:], 0.0)

        @pl.when(polar & (n >= 2))
        def _():
            s = jnp.where(flip, CAP - 1 - (n - 2), n - 2)
            chosen = jnp.clip(polar_rows[first + s] - t * ROWS, 0, ROWS - 1)
            for q in range(SLOT):
                slots[(n - 2) * SLOT + q] = pred[chosen, q]

            for which in range(2):
                for block, segment in enumerate(HELP_SEGMENTS[which]):

                    @pl.when(n == segment + 2)
                    def _():
                        everyone(lambda j: help_send(which, block, j).start())

            for block, segment in enumerate(OWN_SEGMENTS):

                @pl.when(n == segment + 2)
                def _():
                    others(lambda j: own_send(block, i, j).start())
                    own_local(block).start()

        return 0

    def rows_from(lo, hi):
        lax.fori_loop(lo, hi, step, 0)

    @pl.when(polar & jnp.logical_not(flip))
    def _():
        wait_above()

    @pl.when(polar & flip)
    def _():
        wait_below()

    rows_from(jnp.where(polar, 0, 3), 13)

    def ret_own(block, p, j):
        return pltpu.make_async_remote_copy(
            src_ref=result.at[block, p], dst_ref=back.at[units(own_segment(block), j)],
            send_sem=ret_ss, recv_sem=ret_rs,
            device_id=(t, p), device_id_type=MESH,
        )

    def ret_own_local(block):
        return pltpu.make_async_copy(
            result.at[block, i], back.at[units(own_segment(block), i)], ret_rs
        )

    def ret_help(which, block, p, j):
        return pltpu.make_async_remote_copy(
            src_ref=result.at[block, p], dst_ref=back.at[units(3 * block + which, j)],
            send_sem=ret_ss, recv_sem=ret_rs,
            device_id=(host, p), device_id_type=MESH,
        )

    def matmul(wide, head, tail, back_again):
        top = wide.astype(jnp.bfloat16)
        low = (wide - top.astype(jnp.float32)).astype(jnp.bfloat16)
        dims = (((1,), (1 if back_again else 0,)), ((), ()))
        both = lax.dot_general(
            jnp.concatenate([top, low], axis=0), head, dims, preferred_element_type=jnp.float32
        )
        cross = lax.dot_general(top, tail, dims, preferred_element_type=jnp.float32)
        return both[:BATCH] + (both[BATCH:] + cross)

    def band_of(block):
        s = jnp.where(polar, own_segment(block), 3 * block + jnp.where(up, 0, 1))
        return bands[first + jnp.where(flip, CAP - 1 - s, s)]

    def filter_block(block, _):
        await_bytes(pieces.at[block], own_rs.at[block])

        def forward(n, _):
            x = [pieces[block, p, n] for p in range(PARTS)]
            e = [x[p] + x[p + 4] for p in range(4)]
            d = [x[p] - x[p + 4] for p in range(4)]
            here = pl.ds(pl.multiple_of(n * 8, 8), 8)
            minus, plus = HALF * (d[1] - d[3]), HALF * (d[1] + d[3])
            parts = (
                d[0] + minus, -plus - d[2],
                e[0] - e[2], e[3] - e[1],
                d[0] - minus, d[2] - plus,
                (e[0] + e[2]) + (e[1] + e[3]), (e[0] + e[2]) - (e[1] + e[3]),
            )
            for m, part in enumerate(parts):
                spec[here, m * WIDE : (m + 1) * WIDE] = part
            return 0

        lax.fori_loop(0, BLOCK, forward, 0)
        band = band_of(block)
        for m in range(3):
            here = slice(m * 2 * WIDE, (m + 1) * 2 * WIDE)
            waves = matmul(spec[:, here], t_ph[m], t_pl[m], False)
            waves = jnp.where(waves_pair[m] < band, waves * (2.0 / LENGTH), 0.0)
            spec[:, here] = matmul(waves, t_ph[m], t_pl[m], True)
        for m in range(2):
            here = slice((6 + m) * WIDE, (7 + m) * WIDE)
            waves = matmul(spec[:, here], t_oh[m], t_ol[m], False)
            factor = jnp.where(waves_one[m] == 0, 1.0 / LENGTH, 2.0 / LENGTH)
            waves = jnp.where(waves_one[m] < band, waves * factor, 0.0)
            spec[:, here] = matmul(waves, t_oh[m], t_ol[m], True)

        def inverse(n, _):
            here = pl.ds(pl.multiple_of(n * 8, 8), 8)
            r1, i1, r2, i2, r3, i3, z0, z4 = (spec[here, m * WIDE : (m + 1) * WIDE] for m in range(8))
            even, odd = z0 + z4, z0 - z4
            a, b = even + r2, even - r2
            c, d = odd - i2, odd + i2
            rr, ii = r1 + r3, i1 - i3
            u = HALF * ((r1 - r3) - (i1 + i3))
            v = HALF * ((r3 - r1) - (i1 + i3))
            outs = (a + rr, c + u, b - ii, d + v, a - rr, c - u, b + ii, d - v)
            for p, value in enumerate(outs):
                result[block, p, n] = value
            return 0

        lax.fori_loop(0, BLOCK, inverse, 0)

        @pl.when(polar)
        def _():
            others(lambda p: ret_own(block, p, i).start())
            ret_own_local(block).start()

        @pl.when(up)
        def _():
            everyone(lambda p: ret_help(0, block, p, i).start())

        @pl.when(down)
        def _():
            everyone(lambda p: ret_help(1, block, p, i).start())

        return 0

    def pass_on(block):
        await_bytes(relay.at[block], help_rs.at[block])
        others(lambda j: relay_send(block, i, j).start())
        relay_local(block).start()

    for load in loads:
        load.wait()
    blocks = jnp.where(polar | up, MOST, jnp.where(down, len(HELP_SEGMENTS[1]), 0))

    def helped(block, _):
        pass_on(block)

        @pl.when(block > 0)
        def _():
            filter_block(block - 1, 0)

        return 0

    lax.fori_loop(0, jnp.where(helper, blocks, 0), helped, 0)
    ready = jnp.where(helper, blocks - 1, 0)
    lax.fori_loop(ready, jnp.where(helper, blocks, jnp.where(polar, 2, 0)), filter_block, 0)

    @pl.when(polar & jnp.logical_not(flip))
    def _():
        wait_below()

    @pl.when(polar & flip)
    def _():
        wait_above()

    @pl.when(jnp.logical_not(polar))
    def _():
        wait_above()
        wait_below()

    rows_from(ROWS + jnp.where(polar, 3, 0), ROWS + 6)
    lax.fori_loop(2, jnp.where(polar, blocks, 2), filter_block, 0)

    for copy in lon_copies:
        copy.wait_send()

    @pl.when(t < 15)
    def _():
        south_copy.wait_send()

    @pl.when(t > 0)
    def _():
        north_copy.wait_send()

    few = len(HELP_SEGMENTS[1])

    @pl.when(up)
    def _():
        await_bytes(relay.at[:, pl.ds(0, PARTS - 1)], slot_ss)
        await_bytes(result, ret_ss)

    @pl.when(down)
    def _():
        await_bytes(relay.at[pl.ds(0, few), pl.ds(0, PARTS - 1)], slot_ss)
        await_bytes(result.at[pl.ds(0, few)], ret_ss)

    @pl.when(polar)
    def _():
        await_bytes(slots.at[pl.ds(0, UNITS - MOST * BLOCK)], slot_ss)
        await_bytes(result.at[:, pl.ds(0, PARTS - 1)], ret_ss)
        await_bytes(back, ret_rs)


def place(polar_rows, pred, back, out, turned, ready, sems):
    t = lax.axis_index("lat")
    polar, flip = (t < 2) | (t >= 14), t >= 14
    first = jnp.where(t < 2, t, jnp.where(flip, t - 12, 0)) * CAP
    slot_of = []
    for r in range(ROWS):
        before, hit = 0, 0
        for s in range(CAP):
            row = polar_rows[first + s] - t * ROWS
            before = before + jnp.where(row < r, 1, 0)
            hit = hit + jnp.where(row == r, 1, 0)
        s = jnp.minimum(before, CAP - 1)
        slot_of.append((polar & (hit > 0), jnp.where(flip, CAP - 1 - s, s)))

    def leave(at):
        return pltpu.make_async_copy(ready.at[at], out.at[at], sems.at[at])

    def one(at, _):
        f, g = at // GROUPS, lax.rem(at, GROUPS)
        q = g * F + f
        for r in range(ROWS):
            hit, s = slot_of[r]
            value = jnp.where(hit, back[s * SLOT + q], pred[r, q])
            for c in range(3):
                turned[c, pl.ds(r, 8, stride=ROWS), :] = value[:, 128 * c : 128 * (c + 1)]
        ready[at, :, 0:128] = turned[0]
        ready[at, :, 128:256] = turned[1]
        ready[at, :, 256:CELLS] = turned[2, :, 0 : CELLS - 256]
        leave(at).start()
        return 0

    lax.fori_loop(0, QUADS, one, 0)

    def left(at, _):
        leave(at).wait()
        return 0

    lax.fori_loop(0, QUADS, left, 0)


def local(fields, inv_cos, coupling_lon, coupling_lat, polar_rows, bands):
    stay = functools.partial(pltpu.with_memory_space_constraint, memory_space=pltpu.HBM)
    smem, vmem, anywhere = (pl.BlockSpec(memory_space=space) for space in (pltpu.SMEM, pltpu.VMEM, pl.ANY))
    dma = pltpu.SemaphoreType.DMA
    constants = tables()
    f32, bf16 = jnp.float32, jnp.bfloat16
    pred, back = pl.pallas_call(
        kernel,
        out_shape=(
            pltpu.VMEM((ROWS, QUADS, 8, WIDE), f32),
            pltpu.VMEM((UNITS, 8, WIDE), f32),
        ),
        in_specs=[vmem] + [smem] * 5 + [anywhere] * 4 + [vmem] * 3,
        out_specs=(vmem, vmem),
        scratch_shapes=[
            pltpu.VMEM((ROWS + 6, GROUPS, F, 8, WIDE), f32),
            pltpu.VMEM((2, GROUPS, F // 2, 8, 128), f32),
            pltpu.VMEM((2, GROUPS, F // 2, 8, 128), f32),
            pltpu.VMEM((UNITS, 8, WIDE), f32),
            pltpu.VMEM((MOST, PARTS, BLOCK, 8, WIDE), f32),
            pltpu.VMEM((MOST, PARTS, BLOCK, 8, WIDE), f32),
            pltpu.VMEM((MOST, PARTS, BLOCK, 8, WIDE), f32),
            pltpu.VMEM((BATCH, 8 * WIDE), f32),
            pltpu.VMEM((3, 2 * WIDE, 512), bf16),
            pltpu.VMEM((3, 2 * WIDE, 512), bf16),
            pltpu.VMEM((2, WIDE, 256), bf16),
            pltpu.VMEM((2, WIDE, 256), bf16),
            pltpu.VMEM((3, 2, 128, 128), f32),
            pltpu.VMEM((QUADS * 8, WIDE), f32),
            pltpu.VMEM((QUADS * 8, WIDE), f32),
            dma((4,)),
            dma((2,)), dma((2,)), dma((2,)), dma((2,)),
            dma, dma((MOST,)), dma((MOST,)), dma, dma,
        ],
        compiler_params=pltpu.CompilerParams(
            collective_id=0, has_side_effects=True, vmem_limit_bytes=40 * 2**20
        ),
    )(
        stay(fields.reshape(F * LEV * ROWS, CELLS)),
        *(stay(x) for x in (inv_cos, coupling_lon, coupling_lat, polar_rows, bands)),
        *(stay(jnp.asarray(x)) for x in constants),
    )
    out = pl.pallas_call(
        place,
        out_shape=jax.ShapeDtypeStruct((QUADS, 8 * ROWS, CELLS), f32),
        in_specs=[smem, vmem, vmem],
        out_specs=anywhere,
        scratch_shapes=[
            pltpu.VMEM((3, 8 * ROWS, 128), f32),
            pltpu.VMEM((QUADS, 8 * ROWS, CELLS), f32),
            dma((QUADS,)),
        ],
        compiler_params=pltpu.CompilerParams(vmem_limit_bytes=24 * 2**20),
    )(stay(polar_rows), pred, back)
    return out.reshape(F, LEV, ROWS, CELLS)


def solution(mesh):
    return jax.shard_map(
        local,
        mesh=mesh,
        in_specs=(P(None, None, "lat", "lon"), P("lat"), P(), P(), P(), P()),
        out_specs=P(None, None, "lat", "lon"),
        check_vma=False,
    )
```

```python
import functools
import math

import jax
import jax.numpy as jnp
import ml_dtypes
import numpy as np
from jax import lax
from jax.experimental import pallas as pl
from jax.experimental.pallas import tpu as pltpu
from jax.sharding import PartitionSpec as P

MESH = pl.DeviceIdType.MESH
F, LEV, ROWS, CELLS, WIDE = 6, 32, 16, 360, 384
PARTS, LENGTH, KMAX, CAP = 8, 2880, 1024, 14
GROUPS, QUADS = LEV // 8, LEV // 8 * F
SLOT = QUADS
UNITS = CAP * SLOT
BLOCK = 3
SEGMENT = PARTS * BLOCK
HELP_SEGMENTS = ((0, 3, 6, 9), (1, 4, 7, 10))
OWN_SEGMENTS = (2, 5, 8, 11, 12, 13)
OWN, MANY, FEW = (len(entries) for entries in (OWN_SEGMENTS, *HELP_SEGMENTS))
MOST = max(OWN, MANY, FEW)
ROOM = 4
BATCH = 8 * ROOM
HALF = 1.0 / math.sqrt(2.0)


def tables():
    cells = np.arange(CELLS, dtype=np.int64)

    def angles(waves):
        return 2.0 * np.pi * ((cells[:, None] * waves[None, :]) % LENGTH) / LENGTH

    def halves(table):
        wide = np.asarray(table, np.float64)
        head = wide.astype(ml_dtypes.bfloat16)
        return head, (wide - head.astype(np.float64)).astype(ml_dtypes.bfloat16)

    pair = np.zeros((3, 2 * WIDE, 512))
    single = np.zeros((2, WIDE, 256))
    waves_pair = np.zeros((3, 1, 512), np.int32)
    waves_single = np.zeros((2, 1, 256), np.int32)
    for kind in (1, 2, 3):
        waves = kind + 8 * np.arange(-128, 128)
        cos, sin = np.cos(angles(waves)), np.sin(angles(waves))
        pair[kind - 1, :CELLS, :256] = cos
        pair[kind - 1, :CELLS, 256:] = -sin
        pair[kind - 1, WIDE : WIDE + CELLS, :256] = sin
        pair[kind - 1, WIDE : WIDE + CELLS, 256:] = cos
        waves_pair[kind - 1, 0] = np.concatenate([np.abs(waves)] * 2)
    for at, kind in enumerate((0, 4)):
        waves = kind + 8 * np.arange(128)
        single[at, :CELLS, :128] = np.cos(angles(waves))
        single[at, :CELLS, 128:] = -np.sin(angles(waves))
        waves_single[at, 0] = np.concatenate([waves] * 2)
    gaps = np.zeros((WIDE, WIDE))
    for d, factor in ((1, 45.0), (2, -9.0), (3, 1.0)):
        gaps += factor * (np.roll(np.eye(WIDE), d, axis=0) - np.roll(np.eye(WIDE), -d, axis=0))
    return (*halves(pair), *halves(single), waves_pair, waves_single, gaps.astype(ml_dtypes.bfloat16))


def kernel(
    fields, inv_cos, c_lon, c_lat, polar_rows, bands, pair_hi, pair_lo, one_hi, one_lo, waves_pair, waves_one, gap_table,
    pred, back,
    grid, lon_out, lon_in, slots, relay, pieces, result, spec, t_ph, t_pl, t_oh, t_ol, turned, row, along,
    tab_sem, lon_ss, lon_rs, lat_ss, lat_rs, slot_ss, help_rs, own_rs, ret_ss, ret_rs,
):
    t, i = lax.axis_index("lat"), lax.axis_index("lon")
    north, south = t < 2, t >= 14
    polar = north | south
    up = ((t >= 2) & (t < 4)) | ((t >= 12) & (t < 14))
    down = ((t >= 4) & (t < 6)) | ((t >= 10) & (t < 12))
    helper = up | down
    host = jnp.where(polar, t, lax.rem(t + jnp.where(t < 6, 12, 4), 16))
    flip = host >= 14
    first = jnp.where(host < 2, host, jnp.where(flip, host - 12, 0)) * CAP

    loads = [
        pltpu.make_async_copy(src, dst, tab_sem.at[n])
        for n, (src, dst) in enumerate(((pair_hi, t_ph), (pair_lo, t_pl), (one_hi, t_oh), (one_lo, t_ol)))
    ]
    for load in loads:
        load.start()

    barrier = pltpu.get_barrier_semaphore()

    def greet(lat, lon):
        pl.semaphore_signal(barrier, inc=1, device_id=(lat, lon), device_id_type=MESH)

    for k in range(1, PARTS):
        greet(t, lax.rem(i + k, PARTS))

    @pl.when(t > 0)
    def _():
        greet(t - 1, i)

    @pl.when(t < 15)
    def _():
        greet(t + 1, i)

    @pl.when(polar)
    def _():
        for k in range(PARTS):
            greet(lax.rem(t + 4, 16), k)
            greet(lax.rem(t + 12, 16), k)

    @pl.when(helper)
    def _():
        for k in range(PARTS):
            greet(host, k)

    lane = lax.broadcasted_iota(jnp.int32, (8, 128), 1)

    def turn(at, _):
        g, pair = at // (F // 2), lax.rem(at, F // 2)
        low, high = [], []
        for odd in range(2):
            f = 2 * pair + odd
            base = pl.multiple_of(f * LEV * ROWS + g * 128, 128)
            turned[0, odd] = fields[pl.ds(base, 128), 0:128]
            turned[1, odd] = fields[pl.ds(base, 128), 128:256]
            turned[2, odd, :, 0 : CELLS - 256] = fields[pl.ds(base, 128), 256:CELLS]
            for r in range(ROWS):
                k = odd * 16 + r
                tiles = [turned[c, odd, pl.ds(r, 8, stride=ROWS), :] for c in range(3)]
                tiles[2] = jnp.where(lane < CELLS - 256, tiles[2], 0.0)
                for c in range(3):
                    grid[r + 3, g, f, :, 128 * c : 128 * (c + 1)] = tiles[c]
                mine = lane // 4 == k
                low.append(jnp.where(mine, pltpu.roll(tiles[0], 4 * k, axis=1), 0.0))
                high.append(jnp.where(mine, pltpu.roll(tiles[2], (4 * k + 128 - 101) % 128, axis=1), 0.0))
        lon_out[0, g, pair] = functools.reduce(jnp.add, low)
        lon_out[1, g, pair] = functools.reduce(jnp.add, high)
        return 0

    lax.fori_loop(0, GROUPS * F // 2, turn, 0)

    edge = jnp.where(t > 0, 1, 0) + jnp.where(t < 15, 1, 0)
    pl.semaphore_wait(barrier, PARTS - 1 + edge + jnp.where(polar, 2 * PARTS, 0) + jnp.where(helper, PARTS, 0))

    lon_copies = [
        pltpu.make_async_remote_copy(
            src_ref=lon_out.at[side], dst_ref=lon_in.at[side], send_sem=lon_ss.at[side], recv_sem=lon_rs.at[side],
            device_id=(t, lax.rem(i + shift, PARTS)), device_id_type=MESH,
        )
        for side, shift in ((0, PARTS - 1), (1, 1))
    ]
    for copy in lon_copies:
        copy.start()
    south_copy = pltpu.make_async_remote_copy(
        src_ref=grid.at[pl.ds(16, 3)], dst_ref=grid.at[pl.ds(0, 3)], send_sem=lat_ss.at[0], recv_sem=lat_rs.at[0],
        device_id=(jnp.minimum(t + 1, 15), i), device_id_type=MESH,
    )
    north_copy = pltpu.make_async_remote_copy(
        src_ref=grid.at[pl.ds(3, 3)], dst_ref=grid.at[pl.ds(19, 3)], send_sem=lat_ss.at[1], recv_sem=lat_rs.at[1],
        device_id=(jnp.maximum(t - 1, 0), i), device_id_type=MESH,
    )

    @pl.when(t < 15)
    def _():
        south_copy.start()

    @pl.when(t > 0)
    def _():
        north_copy.start()

    def clear(row0):
        def one(r, _):
            for g in range(GROUPS):
                for f in range(F):
                    grid[row0 + r, g, f] = jnp.zeros((8, WIDE), jnp.float32)
            return 0

        lax.fori_loop(0, 3, one, 0)

    @pl.when(t == 0)
    def _():
        clear(0)

    @pl.when(t == 15)
    def _():
        clear(19)

    for copy in lon_copies:
        copy.wait_recv()

    def wait_above():
        @pl.when(t > 0)
        def _():
            south_copy.wait_recv()

    def wait_below():
        @pl.when(t < 15)
        def _():
            north_copy.wait_recv()

    def others(act):
        def one(k, _):
            act(lax.rem(i + k, PARTS))
            return 0

        lax.fori_loop(1, PARTS, one, 0)

    def everyone(act):
        others(act)
        act(i)

    def pick(entries, block):
        chosen = entries[0]
        for n, entry in enumerate(entries):
            chosen = jnp.where(block == n, entry, chosen)
        return chosen

    def await_bytes(ref, sem):
        pltpu.make_async_copy(ref, ref, sem).wait()

    def units(segment, j):
        return pl.ds(segment * SEGMENT + j * BLOCK, BLOCK)

    def own_segment(block):
        return pick(OWN_SEGMENTS, block)

    def help_segment(which, block):
        return pick(HELP_SEGMENTS[which], block)

    def help_send(which, block, j):
        return pltpu.make_async_remote_copy(
            src_ref=slots.at[units(help_segment(which, block), j)], dst_ref=relay.at[block, j],
            send_sem=slot_ss, recv_sem=help_rs.at[block],
            device_id=(lax.rem(t + jnp.where(flip, (4, 12)[which], (12, 4)[which]), 16), i), device_id_type=MESH,
        )

    def own_send(block, p, j):
        return pltpu.make_async_remote_copy(
            src_ref=slots.at[units(own_segment(block), j)], dst_ref=pieces.at[block, p],
            send_sem=slot_ss, recv_sem=own_rs.at[block],
            device_id=(t, j), device_id_type=MESH,
        )

    def own_local(block):
        return pltpu.make_async_copy(
            slots.at[units(own_segment(block), i)], pieces.at[block, i], own_rs.at[block]
        )

    def relay_send(block, p, j):
        return pltpu.make_async_remote_copy(
            src_ref=relay.at[block, j], dst_ref=pieces.at[block, p],
            send_sem=slot_ss, recv_sem=own_rs.at[block],
            device_id=(t, j), device_id_type=MESH,
        )

    def relay_local(block):
        return pltpu.make_async_copy(relay.at[block, i], pieces.at[block, i], own_rs.at[block])

    def step(at, _):
        n = jnp.where(at < ROWS, at, jnp.where(at < ROWS + 3, at - ROWS, at - 6))
        r = jnp.where(flip, ROWS - 1 - n, n)
        scale = inv_cos[r] * (1.0 / 60.0)
        for g in range(GROUPS):
            for f in range(F):
                k = (f % 2) * 16 + r
                east = pltpu.roll(lon_in[0, g, f // 2], lax.rem(104 + 128 - 4 * k, 128), axis=1)
                west = pltpu.roll(lon_in[1, g, f // 2], lax.rem(125 + 128 - 4 * k, 128), axis=1)
                halo = jnp.where((lane >= 104) & (lane < 107), east, jnp.where(lane >= 125, west, 0.0))
                here = slice((g * F + f) * 8, (g * F + f + 1) * 8)
                row[here, 0:256] = grid[r + 3, g, f, :, 0:256]
                row[here, 256:WIDE] = grid[r + 3, g, f, :, 256:WIDE] + halo
        top = row[...].astype(jnp.bfloat16)
        low = (row[...] - top.astype(jnp.float32)).astype(jnp.bfloat16)
        both = jnp.dot(
            jnp.concatenate([top, low], axis=0), gap_table[...], preferred_element_type=jnp.float32
        )
        along[...] = (both[: QUADS * 8] + both[QUADS * 8 :]) * scale

        for g in range(GROUPS):
            along_lat, along_lon = [], []
            for f in range(F):

                def at_row(d):
                    return grid[r + 3 + d, g, f]

                along_lat.append(
                    (45.0 * (at_row(1) - at_row(-1)) - 9.0 * (at_row(2) - at_row(-2)) + (at_row(3) - at_row(-3)))
                    * (1.0 / 60.0)
                )
                along_lon.append(along[(g * F + f) * 8 : (g * F + f + 1) * 8, :])
            for f in range(F):
                total = grid[r + 3, g, f]
                for h in range(F):
                    total = total + c_lon[f, h] * along_lon[h] + c_lat[f, h] * along_lat[h]
                pred[r, g * F + f, :, 0:256] = total[:, 0:256]
                pred[r, g * F + f, :, 256:WIDE] = jnp.where(lane < CELLS - 256, total[:, 256:], 0.0)

        @pl.when(polar & (n >= 2))
        def _():
            s = jnp.where(flip, CAP - 1 - (n - 2), n - 2)
            chosen = jnp.clip(polar_rows[first + s] - t * ROWS, 0, ROWS - 1)
            for q in range(SLOT):
                slots[(n - 2) * SLOT + q] = pred[chosen, q]

            for which in range(2):
                for block, segment in enumerate(HELP_SEGMENTS[which]):

                    @pl.when(n == segment + 2)
                    def _():
                        everyone(lambda j: help_send(which, block, j).start())

            for block, segment in enumerate(OWN_SEGMENTS):

                @pl.when(n == segment + 2)
                def _():
                    others(lambda j: own_send(block, i, j).start())
                    own_local(block).start()

        return 0

    def rows_from(lo, hi):
        lax.fori_loop(lo, hi, step, 0)

    @pl.when(polar & jnp.logical_not(flip))
    def _():
        wait_above()

    @pl.when(polar & flip)
    def _():
        wait_below()

    rows_from(jnp.where(polar, 0, 3), 13)

    def ret_own(block, p, j):
        return pltpu.make_async_remote_copy(
            src_ref=result.at[block, p], dst_ref=back.at[units(own_segment(block), j)],
            send_sem=ret_ss, recv_sem=ret_rs,
            device_id=(t, p), device_id_type=MESH,
        )

    def ret_own_local(block):
        return pltpu.make_async_copy(
            result.at[block, i], back.at[units(own_segment(block), i)], ret_rs
        )

    def ret_help(which, block, p, j):
        return pltpu.make_async_remote_copy(
            src_ref=result.at[block, p], dst_ref=back.at[units(help_segment(which, block), j)],
            send_sem=ret_ss, recv_sem=ret_rs,
            device_id=(host, p), device_id_type=MESH,
        )

    def matmul(wide, head, tail, back_again):
        top = wide.astype(jnp.bfloat16)
        low = (wide - top.astype(jnp.float32)).astype(jnp.bfloat16)
        dims = (((1,), (1 if back_again else 0,)), ((), ()))
        both = lax.dot_general(
            jnp.concatenate([top, low], axis=0), head, dims, preferred_element_type=jnp.float32
        )
        cross = lax.dot_general(top, tail, dims, preferred_element_type=jnp.float32)
        return both[:BATCH] + (both[BATCH:] + cross)

    def band_of(block):
        s = jnp.where(polar, own_segment(block), jnp.where(up, help_segment(0, block), help_segment(1, block)))
        return bands[first + jnp.where(flip, CAP - 1 - s, s)]

    def filter_block(block, _):
        await_bytes(pieces.at[block], own_rs.at[block])

        def forward(n, _):
            x = [pieces[block, p, n] for p in range(PARTS)]
            e = [x[p] + x[p + 4] for p in range(4)]
            d = [x[p] - x[p + 4] for p in range(4)]
            here = pl.ds(pl.multiple_of(n * 8, 8), 8)
            minus, plus = HALF * (d[1] - d[3]), HALF * (d[1] + d[3])
            parts = (
                d[0] + minus, -plus - d[2],
                e[0] - e[2], e[3] - e[1],
                d[0] - minus, d[2] - plus,
                (e[0] + e[2]) + (e[1] + e[3]), (e[0] + e[2]) - (e[1] + e[3]),
            )
            for m, part in enumerate(parts):
                spec[here, m * WIDE : (m + 1) * WIDE] = part
            return 0

        lax.fori_loop(0, BLOCK, forward, 0)
        band = band_of(block)
        for m in range(3):
            here = slice(m * 2 * WIDE, (m + 1) * 2 * WIDE)
            waves = matmul(spec[:, here], t_ph[m], t_pl[m], False)
            waves = jnp.where(waves_pair[m] < band, waves * (2.0 / LENGTH), 0.0)
            spec[:, here] = matmul(waves, t_ph[m], t_pl[m], True)
        for m in range(2):
            here = slice((6 + m) * WIDE, (7 + m) * WIDE)
            waves = matmul(spec[:, here], t_oh[m], t_ol[m], False)
            factor = jnp.where(waves_one[m] == 0, 1.0 / LENGTH, 2.0 / LENGTH)
            waves = jnp.where(waves_one[m] < band, waves * factor, 0.0)
            spec[:, here] = matmul(waves, t_oh[m], t_ol[m], True)

        def inverse(n, _):
            here = pl.ds(pl.multiple_of(n * 8, 8), 8)
            r1, i1, r2, i2, r3, i3, z0, z4 = (spec[here, m * WIDE : (m + 1) * WIDE] for m in range(8))
            even, odd = z0 + z4, z0 - z4
            a, b = even + r2, even - r2
            c, d = odd - i2, odd + i2
            rr, ii = r1 + r3, i1 - i3
            u = HALF * ((r1 - r3) - (i1 + i3))
            v = HALF * ((r3 - r1) - (i1 + i3))
            outs = (a + rr, c + u, b - ii, d + v, a - rr, c - u, b + ii, d - v)
            for p, value in enumerate(outs):
                result[block, p, n] = value
            return 0

        lax.fori_loop(0, BLOCK, inverse, 0)

        @pl.when(polar)
        def _():
            others(lambda p: ret_own(block, p, i).start())
            ret_own_local(block).start()

        @pl.when(up)
        def _():
            everyone(lambda p: ret_help(0, block, p, i).start())

        @pl.when(down)
        def _():
            everyone(lambda p: ret_help(1, block, p, i).start())

        return 0

    def pass_on(block):
        await_bytes(relay.at[block], help_rs.at[block])
        others(lambda j: relay_send(block, i, j).start())
        relay_local(block).start()

    for load in loads:
        load.wait()
    blocks = jnp.where(polar, OWN, jnp.where(up, MANY, jnp.where(down, FEW, 0)))

    def helped(block, _):
        pass_on(block)

        @pl.when(block > 0)
        def _():
            filter_block(block - 1, 0)

        return 0

    lax.fori_loop(0, jnp.where(helper, blocks, 0), helped, 0)
    ready = jnp.where(helper, blocks - 1, 0)
    lax.fori_loop(ready, jnp.where(helper, blocks, jnp.where(polar, 2, 0)), filter_block, 0)

    @pl.when(polar & jnp.logical_not(flip))
    def _():
        wait_below()

    @pl.when(polar & flip)
    def _():
        wait_above()

    @pl.when(jnp.logical_not(polar))
    def _():
        wait_above()
        wait_below()

    rows_from(ROWS + jnp.where(polar, 3, 0), ROWS + 6)
    lax.fori_loop(2, jnp.where(polar, blocks, 2), filter_block, 0)

    for copy in lon_copies:
        copy.wait_send()

    @pl.when(t < 15)
    def _():
        south_copy.wait_send()

    @pl.when(t > 0)
    def _():
        north_copy.wait_send()

    @pl.when(up)
    def _():
        await_bytes(relay.at[pl.ds(0, MANY), pl.ds(0, PARTS - 1)], slot_ss)
        await_bytes(result.at[pl.ds(0, MANY)], ret_ss)

    @pl.when(down)
    def _():
        await_bytes(relay.at[pl.ds(0, FEW), pl.ds(0, PARTS - 1)], slot_ss)
        await_bytes(result.at[pl.ds(0, FEW)], ret_ss)

    @pl.when(polar)
    def _():
        await_bytes(slots.at[pl.ds(0, UNITS - OWN * BLOCK)], slot_ss)
        await_bytes(result.at[pl.ds(0, OWN), pl.ds(0, PARTS - 1)], ret_ss)
        await_bytes(back, ret_rs)


def place(polar_rows, pred, back, out, turned, ready, sems):
    t = lax.axis_index("lat")
    polar, flip = (t < 2) | (t >= 14), t >= 14
    first = jnp.where(t < 2, t, jnp.where(flip, t - 12, 0)) * CAP
    slot_of = []
    for r in range(ROWS):
        before, hit = 0, 0
        for s in range(CAP):
            row = polar_rows[first + s] - t * ROWS
            before = before + jnp.where(row < r, 1, 0)
            hit = hit + jnp.where(row == r, 1, 0)
        s = jnp.minimum(before, CAP - 1)
        slot_of.append((polar & (hit > 0), jnp.where(flip, CAP - 1 - s, s)))

    def leave(at):
        return pltpu.make_async_copy(ready.at[at], out.at[at], sems.at[at])

    def one(at, _):
        f, g = at // GROUPS, lax.rem(at, GROUPS)
        q = g * F + f
        for r in range(ROWS):
            hit, s = slot_of[r]
            value = jnp.where(hit, back[s * SLOT + q], pred[r, q])
            for c in range(3):
                turned[c, pl.ds(r, 8, stride=ROWS), :] = value[:, 128 * c : 128 * (c + 1)]
        ready[at, :, 0:128] = turned[0]
        ready[at, :, 128:256] = turned[1]
        ready[at, :, 256:CELLS] = turned[2, :, 0 : CELLS - 256]
        leave(at).start()
        return 0

    lax.fori_loop(0, QUADS, one, 0)

    def left(at, _):
        leave(at).wait()
        return 0

    lax.fori_loop(0, QUADS, left, 0)


def local(fields, inv_cos, coupling_lon, coupling_lat, polar_rows, bands):
    stay = functools.partial(pltpu.with_memory_space_constraint, memory_space=pltpu.HBM)
    smem, vmem, anywhere = (pl.BlockSpec(memory_space=space) for space in (pltpu.SMEM, pltpu.VMEM, pl.ANY))
    dma = pltpu.SemaphoreType.DMA
    constants = tables()
    f32, bf16 = jnp.float32, jnp.bfloat16
    pred, back = pl.pallas_call(
        kernel,
        out_shape=(
            pltpu.VMEM((ROWS, QUADS, 8, WIDE), f32),
            pltpu.VMEM((UNITS, 8, WIDE), f32),
        ),
        in_specs=[vmem] + [smem] * 5 + [anywhere] * 4 + [vmem] * 3,
        out_specs=(vmem, vmem),
        scratch_shapes=[
            pltpu.VMEM((ROWS + 6, GROUPS, F, 8, WIDE), f32),
            pltpu.VMEM((2, GROUPS, F // 2, 8, 128), f32),
            pltpu.VMEM((2, GROUPS, F // 2, 8, 128), f32),
            pltpu.VMEM((UNITS, 8, WIDE), f32),
            pltpu.VMEM((MOST, PARTS, BLOCK, 8, WIDE), f32),
            pltpu.VMEM((MOST, PARTS, BLOCK, 8, WIDE), f32),
            pltpu.VMEM((MOST, PARTS, BLOCK, 8, WIDE), f32),
            pltpu.VMEM((BATCH, 8 * WIDE), f32),
            pltpu.VMEM((3, 2 * WIDE, 512), bf16),
            pltpu.VMEM((3, 2 * WIDE, 512), bf16),
            pltpu.VMEM((2, WIDE, 256), bf16),
            pltpu.VMEM((2, WIDE, 256), bf16),
            pltpu.VMEM((3, 2, 128, 128), f32),
            pltpu.VMEM((QUADS * 8, WIDE), f32),
            pltpu.VMEM((QUADS * 8, WIDE), f32),
            dma((4,)),
            dma((2,)), dma((2,)), dma((2,)), dma((2,)),
            dma, dma((MOST,)), dma((MOST,)), dma, dma,
        ],
        compiler_params=pltpu.CompilerParams(
            collective_id=0, has_side_effects=True, vmem_limit_bytes=40 * 2**20
        ),
    )(
        stay(fields.reshape(F * LEV * ROWS, CELLS)),
        *(stay(x) for x in (inv_cos, coupling_lon, coupling_lat, polar_rows, bands)),
        *(stay(jnp.asarray(x)) for x in constants),
    )
    out = pl.pallas_call(
        place,
        out_shape=jax.ShapeDtypeStruct((QUADS, 8 * ROWS, CELLS), f32),
        in_specs=[smem, vmem, vmem],
        out_specs=anywhere,
        scratch_shapes=[
            pltpu.VMEM((3, 8 * ROWS, 128), f32),
            pltpu.VMEM((QUADS, 8 * ROWS, CELLS), f32),
            dma((QUADS,)),
        ],
        compiler_params=pltpu.CompilerParams(vmem_limit_bytes=24 * 2**20),
    )(stay(polar_rows), pred, back)
    return out.reshape(F, LEV, ROWS, CELLS)


def solution(mesh):
    return jax.shard_map(
        local,
        mesh=mesh,
        in_specs=(P(None, None, "lat", "lon"), P("lat"), P(), P(), P(), P()),
        out_specs=P(None, None, "lat", "lon"),
        check_vma=False,
    )
```

```python
import functools
import math

import jax
import jax.numpy as jnp
import ml_dtypes
import numpy as np
from jax import lax
from jax.experimental import pallas as pl
from jax.experimental.pallas import tpu as pltpu
from jax.sharding import PartitionSpec as P

MESH = pl.DeviceIdType.MESH
F, LEV, ROWS, CELLS, WIDE = 6, 32, 16, 360, 384
PARTS, LENGTH, KMAX, CAP = 8, 2880, 1024, 14
GROUPS, QUADS = LEV // 8, LEV // 8 * F
SLOT = QUADS
UNITS = CAP * SLOT
BLOCK = 3
SEGMENT = PARTS * BLOCK
HELP_SEGMENTS = ((0, 3, 6, 9), (1, 4, 7, 10))
OWN_SEGMENTS = (2, 5, 8, 11, 12, 13)
OWN, MANY, FEW = (len(entries) for entries in (OWN_SEGMENTS, *HELP_SEGMENTS))
MOST = max(OWN, MANY, FEW)
ROOM = 4
BATCH = 8 * ROOM
HALF = 1.0 / math.sqrt(2.0)


def tables():
    cells = np.arange(CELLS, dtype=np.int64)

    def angles(waves):
        return 2.0 * np.pi * ((cells[:, None] * waves[None, :]) % LENGTH) / LENGTH

    def halves(table):
        wide = np.asarray(table, np.float64)
        head = wide.astype(ml_dtypes.bfloat16)
        return head, (wide - head.astype(np.float64)).astype(ml_dtypes.bfloat16)

    pair = np.zeros((3, 2 * WIDE, 512))
    single = np.zeros((2, WIDE, 256))
    waves_pair = np.zeros((3, 1, 512), np.int32)
    waves_single = np.zeros((2, 1, 256), np.int32)
    for kind in (1, 2, 3):
        waves = kind + 8 * np.arange(-128, 128)
        cos, sin = np.cos(angles(waves)), np.sin(angles(waves))
        pair[kind - 1, :CELLS, :256] = cos
        pair[kind - 1, :CELLS, 256:] = -sin
        pair[kind - 1, WIDE : WIDE + CELLS, :256] = sin
        pair[kind - 1, WIDE : WIDE + CELLS, 256:] = cos
        waves_pair[kind - 1, 0] = np.concatenate([np.abs(waves)] * 2)
    for at, kind in enumerate((0, 4)):
        waves = kind + 8 * np.arange(128)
        single[at, :CELLS, :128] = np.cos(angles(waves))
        single[at, :CELLS, 128:] = -np.sin(angles(waves))
        waves_single[at, 0] = np.concatenate([waves] * 2)
    gaps = np.zeros((WIDE, WIDE))
    for d, factor in ((1, 45.0), (2, -9.0), (3, 1.0)):
        gaps += factor * (np.roll(np.eye(WIDE), d, axis=0) - np.roll(np.eye(WIDE), -d, axis=0))
    return (*halves(pair), *halves(single), waves_pair, waves_single, gaps.astype(ml_dtypes.bfloat16))


def kernel(
    arriving, inv_cos, c_lon, c_lat, polar_rows, bands, pair_hi, pair_lo, one_hi, one_lo, waves_pair, waves_one, gap_table,
    pred, back,
    grid, lon_out, lon_in, slots, relay, pieces, result, spec, t_ph, t_pl, t_oh, t_ol, turned, row, along, fields, in_sem,
    tab_sem, lon_ss, lon_rs, lat_ss, lat_rs, slot_ss, help_rs, own_rs, ret_ss, ret_rs,
):
    t, i = lax.axis_index("lat"), lax.axis_index("lon")
    north, south = t < 2, t >= 14
    polar = north | south
    up = ((t >= 2) & (t < 4)) | ((t >= 12) & (t < 14))
    down = ((t >= 4) & (t < 6)) | ((t >= 10) & (t < 12))
    helper = up | down
    host = jnp.where(polar, t, lax.rem(t + jnp.where(t < 6, 12, 4), 16))
    flip = host >= 14
    first = jnp.where(host < 2, host, jnp.where(flip, host - 12, 0)) * CAP

    loads = [
        pltpu.make_async_copy(src, dst, tab_sem.at[n])
        for n, (src, dst) in enumerate(((pair_hi, t_ph), (pair_lo, t_pl), (one_hi, t_oh), (one_lo, t_ol)))
    ]
    def enter(at):
        rows = pl.ds(pl.multiple_of(at * 128, 128), 128)
        return pltpu.make_async_copy(arriving.at[rows], fields.at[rows], in_sem.at[at])

    for g in range(GROUPS):
        for f in range(F):
            enter(f * GROUPS + g).start()
    for load in loads:
        load.start()

    barrier = pltpu.get_barrier_semaphore()

    def greet(lat, lon):
        pl.semaphore_signal(barrier, inc=1, device_id=(lat, lon), device_id_type=MESH)

    for k in range(1, PARTS):
        greet(t, lax.rem(i + k, PARTS))

    @pl.when(t > 0)
    def _():
        greet(t - 1, i)

    @pl.when(t < 15)
    def _():
        greet(t + 1, i)

    @pl.when(polar)
    def _():
        for k in range(PARTS):
            greet(lax.rem(t + 4, 16), k)
            greet(lax.rem(t + 12, 16), k)

    @pl.when(helper)
    def _():
        for k in range(PARTS):
            greet(host, k)

    lane = lax.broadcasted_iota(jnp.int32, (8, 128), 1)

    def turn(at, _):
        g, pair = at // (F // 2), lax.rem(at, F // 2)
        low, high = [], []
        for odd in range(2):
            f = 2 * pair + odd
            base = pl.multiple_of(f * LEV * ROWS + g * 128, 128)
            enter(f * GROUPS + g).wait()
            turned[0, odd] = fields[pl.ds(base, 128), 0:128]
            turned[1, odd] = fields[pl.ds(base, 128), 128:256]
            turned[2, odd, :, 0 : CELLS - 256] = fields[pl.ds(base, 128), 256:CELLS]
            for r in range(ROWS):
                k = odd * 16 + r
                tiles = [turned[c, odd, pl.ds(r, 8, stride=ROWS), :] for c in range(3)]
                tiles[2] = jnp.where(lane < CELLS - 256, tiles[2], 0.0)
                for c in range(3):
                    grid[r + 3, g, f, :, 128 * c : 128 * (c + 1)] = tiles[c]
                mine = lane // 4 == k
                low.append(jnp.where(mine, pltpu.roll(tiles[0], 4 * k, axis=1), 0.0))
                high.append(jnp.where(mine, pltpu.roll(tiles[2], (4 * k + 128 - 101) % 128, axis=1), 0.0))
        lon_out[0, g, pair] = functools.reduce(jnp.add, low)
        lon_out[1, g, pair] = functools.reduce(jnp.add, high)
        return 0

    lax.fori_loop(0, GROUPS * F // 2, turn, 0)

    edge = jnp.where(t > 0, 1, 0) + jnp.where(t < 15, 1, 0)
    pl.semaphore_wait(barrier, PARTS - 1 + edge + jnp.where(polar, 2 * PARTS, 0) + jnp.where(helper, PARTS, 0))

    lon_copies = [
        pltpu.make_async_remote_copy(
            src_ref=lon_out.at[side], dst_ref=lon_in.at[side], send_sem=lon_ss.at[side], recv_sem=lon_rs.at[side],
            device_id=(t, lax.rem(i + shift, PARTS)), device_id_type=MESH,
        )
        for side, shift in ((0, PARTS - 1), (1, 1))
    ]
    for copy in lon_copies:
        copy.start()
    south_copy = pltpu.make_async_remote_copy(
        src_ref=grid.at[pl.ds(16, 3)], dst_ref=grid.at[pl.ds(0, 3)], send_sem=lat_ss.at[0], recv_sem=lat_rs.at[0],
        device_id=(jnp.minimum(t + 1, 15), i), device_id_type=MESH,
    )
    north_copy = pltpu.make_async_remote_copy(
        src_ref=grid.at[pl.ds(3, 3)], dst_ref=grid.at[pl.ds(19, 3)], send_sem=lat_ss.at[1], recv_sem=lat_rs.at[1],
        device_id=(jnp.maximum(t - 1, 0), i), device_id_type=MESH,
    )

    @pl.when(t < 15)
    def _():
        south_copy.start()

    @pl.when(t > 0)
    def _():
        north_copy.start()

    def clear(row0):
        def one(r, _):
            for g in range(GROUPS):
                for f in range(F):
                    grid[row0 + r, g, f] = jnp.zeros((8, WIDE), jnp.float32)
            return 0

        lax.fori_loop(0, 3, one, 0)

    @pl.when(t == 0)
    def _():
        clear(0)

    @pl.when(t == 15)
    def _():
        clear(19)

    for copy in lon_copies:
        copy.wait_recv()

    def wait_above():
        @pl.when(t > 0)
        def _():
            south_copy.wait_recv()

    def wait_below():
        @pl.when(t < 15)
        def _():
            north_copy.wait_recv()

    def others(act):
        def one(k, _):
            act(lax.rem(i + k, PARTS))
            return 0

        lax.fori_loop(1, PARTS, one, 0)

    def everyone(act):
        others(act)
        act(i)

    def pick(entries, block):
        chosen = entries[0]
        for n, entry in enumerate(entries):
            chosen = jnp.where(block == n, entry, chosen)
        return chosen

    def await_bytes(ref, sem):
        pltpu.make_async_copy(ref, ref, sem).wait()

    def units(segment, j):
        return pl.ds(segment * SEGMENT + j * BLOCK, BLOCK)

    def own_segment(block):
        return pick(OWN_SEGMENTS, block)

    def help_segment(which, block):
        return pick(HELP_SEGMENTS[which], block)

    def help_send(which, block, j):
        return pltpu.make_async_remote_copy(
            src_ref=slots.at[units(help_segment(which, block), j)], dst_ref=relay.at[block, j],
            send_sem=slot_ss, recv_sem=help_rs.at[block],
            device_id=(lax.rem(t + jnp.where(flip, (4, 12)[which], (12, 4)[which]), 16), i), device_id_type=MESH,
        )

    def own_send(block, p, j):
        return pltpu.make_async_remote_copy(
            src_ref=slots.at[units(own_segment(block), j)], dst_ref=pieces.at[block, p],
            send_sem=slot_ss, recv_sem=own_rs.at[block],
            device_id=(t, j), device_id_type=MESH,
        )

    def own_local(block):
        return pltpu.make_async_copy(
            slots.at[units(own_segment(block), i)], pieces.at[block, i], own_rs.at[block]
        )

    def relay_send(block, p, j):
        return pltpu.make_async_remote_copy(
            src_ref=relay.at[block, j], dst_ref=pieces.at[block, p],
            send_sem=slot_ss, recv_sem=own_rs.at[block],
            device_id=(t, j), device_id_type=MESH,
        )

    def relay_local(block):
        return pltpu.make_async_copy(relay.at[block, i], pieces.at[block, i], own_rs.at[block])

    def step(at, _):
        n = jnp.where(at < ROWS, at, jnp.where(at < ROWS + 3, at - ROWS, at - 6))
        r = jnp.where(flip, ROWS - 1 - n, n)
        scale = inv_cos[r] * (1.0 / 60.0)
        for g in range(GROUPS):
            for f in range(F):
                k = (f % 2) * 16 + r
                east = pltpu.roll(lon_in[0, g, f // 2], lax.rem(104 + 128 - 4 * k, 128), axis=1)
                west = pltpu.roll(lon_in[1, g, f // 2], lax.rem(125 + 128 - 4 * k, 128), axis=1)
                halo = jnp.where((lane >= 104) & (lane < 107), east, jnp.where(lane >= 125, west, 0.0))
                here = slice((g * F + f) * 8, (g * F + f + 1) * 8)
                row[here, 0:256] = grid[r + 3, g, f, :, 0:256]
                row[here, 256:WIDE] = grid[r + 3, g, f, :, 256:WIDE] + halo
        top = row[...].astype(jnp.bfloat16)
        low = (row[...] - top.astype(jnp.float32)).astype(jnp.bfloat16)
        both = jnp.dot(
            jnp.concatenate([top, low], axis=0), gap_table[...], preferred_element_type=jnp.float32
        )
        along[...] = (both[: QUADS * 8] + both[QUADS * 8 :]) * scale

        for g in range(GROUPS):
            along_lat, along_lon = [], []
            for f in range(F):

                def at_row(d):
                    return grid[r + 3 + d, g, f]

                along_lat.append(
                    (45.0 * (at_row(1) - at_row(-1)) - 9.0 * (at_row(2) - at_row(-2)) + (at_row(3) - at_row(-3)))
                    * (1.0 / 60.0)
                )
                along_lon.append(along[(g * F + f) * 8 : (g * F + f + 1) * 8, :])
            for f in range(F):
                total = grid[r + 3, g, f]
                for h in range(F):
                    total = total + c_lon[f, h] * along_lon[h] + c_lat[f, h] * along_lat[h]
                pred[r, g * F + f, :, 0:256] = total[:, 0:256]
                pred[r, g * F + f, :, 256:WIDE] = jnp.where(lane < CELLS - 256, total[:, 256:], 0.0)

        @pl.when(polar & (n >= 2))
        def _():
            s = jnp.where(flip, CAP - 1 - (n - 2), n - 2)
            chosen = jnp.clip(polar_rows[first + s] - t * ROWS, 0, ROWS - 1)
            for q in range(SLOT):
                slots[(n - 2) * SLOT + q] = pred[chosen, q]

            for which in range(2):
                for block, segment in enumerate(HELP_SEGMENTS[which]):

                    @pl.when(n == segment + 2)
                    def _():
                        everyone(lambda j: help_send(which, block, j).start())

            for block, segment in enumerate(OWN_SEGMENTS):

                @pl.when(n == segment + 2)
                def _():
                    others(lambda j: own_send(block, i, j).start())
                    own_local(block).start()

        return 0

    def rows_from(lo, hi):
        lax.fori_loop(lo, hi, step, 0)

    @pl.when(polar & jnp.logical_not(flip))
    def _():
        wait_above()

    @pl.when(polar & flip)
    def _():
        wait_below()

    rows_from(jnp.where(polar, 0, 3), 13)

    def ret_own(block, p, j):
        return pltpu.make_async_remote_copy(
            src_ref=result.at[block, p], dst_ref=back.at[units(own_segment(block), j)],
            send_sem=ret_ss, recv_sem=ret_rs,
            device_id=(t, p), device_id_type=MESH,
        )

    def ret_own_local(block):
        return pltpu.make_async_copy(
            result.at[block, i], back.at[units(own_segment(block), i)], ret_rs
        )

    def ret_help(which, block, p, j):
        return pltpu.make_async_remote_copy(
            src_ref=result.at[block, p], dst_ref=back.at[units(help_segment(which, block), j)],
            send_sem=ret_ss, recv_sem=ret_rs,
            device_id=(host, p), device_id_type=MESH,
        )

    def matmul(wide, head, tail, back_again):
        top = wide.astype(jnp.bfloat16)
        low = (wide - top.astype(jnp.float32)).astype(jnp.bfloat16)
        dims = (((1,), (1 if back_again else 0,)), ((), ()))
        both = lax.dot_general(
            jnp.concatenate([top, low], axis=0), head, dims, preferred_element_type=jnp.float32
        )
        cross = lax.dot_general(top, tail, dims, preferred_element_type=jnp.float32)
        return both[:BATCH] + (both[BATCH:] + cross)

    def band_of(block):
        s = jnp.where(polar, own_segment(block), jnp.where(up, help_segment(0, block), help_segment(1, block)))
        return bands[first + jnp.where(flip, CAP - 1 - s, s)]

    def filter_block(block, _):
        await_bytes(pieces.at[block], own_rs.at[block])

        def forward(n, _):
            x = [pieces[block, p, n] for p in range(PARTS)]
            e = [x[p] + x[p + 4] for p in range(4)]
            d = [x[p] - x[p + 4] for p in range(4)]
            here = pl.ds(pl.multiple_of(n * 8, 8), 8)
            minus, plus = HALF * (d[1] - d[3]), HALF * (d[1] + d[3])
            parts = (
                d[0] + minus, -plus - d[2],
                e[0] - e[2], e[3] - e[1],
                d[0] - minus, d[2] - plus,
                (e[0] + e[2]) + (e[1] + e[3]), (e[0] + e[2]) - (e[1] + e[3]),
            )
            for m, part in enumerate(parts):
                spec[here, m * WIDE : (m + 1) * WIDE] = part
            return 0

        lax.fori_loop(0, BLOCK, forward, 0)
        band = band_of(block)
        for m in range(3):
            here = slice(m * 2 * WIDE, (m + 1) * 2 * WIDE)
            waves = matmul(spec[:, here], t_ph[m], t_pl[m], False)
            waves = jnp.where(waves_pair[m] < band, waves * (2.0 / LENGTH), 0.0)
            spec[:, here] = matmul(waves, t_ph[m], t_pl[m], True)
        for m in range(2):
            here = slice((6 + m) * WIDE, (7 + m) * WIDE)
            waves = matmul(spec[:, here], t_oh[m], t_ol[m], False)
            factor = jnp.where(waves_one[m] == 0, 1.0 / LENGTH, 2.0 / LENGTH)
            waves = jnp.where(waves_one[m] < band, waves * factor, 0.0)
            spec[:, here] = matmul(waves, t_oh[m], t_ol[m], True)

        def inverse(n, _):
            here = pl.ds(pl.multiple_of(n * 8, 8), 8)
            r1, i1, r2, i2, r3, i3, z0, z4 = (spec[here, m * WIDE : (m + 1) * WIDE] for m in range(8))
            even, odd = z0 + z4, z0 - z4
            a, b = even + r2, even - r2
            c, d = odd - i2, odd + i2
            rr, ii = r1 + r3, i1 - i3
            u = HALF * ((r1 - r3) - (i1 + i3))
            v = HALF * ((r3 - r1) - (i1 + i3))
            outs = (a + rr, c + u, b - ii, d + v, a - rr, c - u, b + ii, d - v)
            for p, value in enumerate(outs):
                result[block, p, n] = value
            return 0

        lax.fori_loop(0, BLOCK, inverse, 0)

        @pl.when(polar)
        def _():
            others(lambda p: ret_own(block, p, i).start())
            ret_own_local(block).start()

        @pl.when(up)
        def _():
            everyone(lambda p: ret_help(0, block, p, i).start())

        @pl.when(down)
        def _():
            everyone(lambda p: ret_help(1, block, p, i).start())

        return 0

    def pass_on(block):
        await_bytes(relay.at[block], help_rs.at[block])
        others(lambda j: relay_send(block, i, j).start())
        relay_local(block).start()

    for load in loads:
        load.wait()
    blocks = jnp.where(polar, OWN, jnp.where(up, MANY, jnp.where(down, FEW, 0)))

    def helped(block, _):
        pass_on(block)

        @pl.when(block > 0)
        def _():
            filter_block(block - 1, 0)

        return 0

    lax.fori_loop(0, jnp.where(helper, blocks, 0), helped, 0)
    ready = jnp.where(helper, blocks - 1, 0)
    lax.fori_loop(ready, jnp.where(helper, blocks, jnp.where(polar, 2, 0)), filter_block, 0)

    @pl.when(polar & jnp.logical_not(flip))
    def _():
        wait_below()

    @pl.when(polar & flip)
    def _():
        wait_above()

    @pl.when(jnp.logical_not(polar))
    def _():
        wait_above()
        wait_below()

    rows_from(ROWS + jnp.where(polar, 3, 0), ROWS + 6)
    lax.fori_loop(2, jnp.where(polar, blocks, 2), filter_block, 0)

    for copy in lon_copies:
        copy.wait_send()

    @pl.when(t < 15)
    def _():
        south_copy.wait_send()

    @pl.when(t > 0)
    def _():
        north_copy.wait_send()

    @pl.when(up)
    def _():
        await_bytes(relay.at[pl.ds(0, MANY), pl.ds(0, PARTS - 1)], slot_ss)
        await_bytes(result.at[pl.ds(0, MANY)], ret_ss)

    @pl.when(down)
    def _():
        await_bytes(relay.at[pl.ds(0, FEW), pl.ds(0, PARTS - 1)], slot_ss)
        await_bytes(result.at[pl.ds(0, FEW)], ret_ss)

    @pl.when(polar)
    def _():
        await_bytes(slots.at[pl.ds(0, UNITS - OWN * BLOCK)], slot_ss)
        await_bytes(result.at[pl.ds(0, OWN), pl.ds(0, PARTS - 1)], ret_ss)
        await_bytes(back, ret_rs)


def place(polar_rows, pred, back, out, turned, ready, sems):
    t = lax.axis_index("lat")
    polar, flip = (t < 2) | (t >= 14), t >= 14
    first = jnp.where(t < 2, t, jnp.where(flip, t - 12, 0)) * CAP
    slot_of = []
    for r in range(ROWS):
        before, hit = 0, 0
        for s in range(CAP):
            row = polar_rows[first + s] - t * ROWS
            before = before + jnp.where(row < r, 1, 0)
            hit = hit + jnp.where(row == r, 1, 0)
        s = jnp.minimum(before, CAP - 1)
        slot_of.append((polar & (hit > 0), jnp.where(flip, CAP - 1 - s, s)))

    def leave(at):
        return pltpu.make_async_copy(ready.at[at], out.at[at], sems.at[at])

    def one(at, _):
        f, g = at // GROUPS, lax.rem(at, GROUPS)
        q = g * F + f
        for r in range(ROWS):
            hit, s = slot_of[r]
            value = jnp.where(hit, back[s * SLOT + q], pred[r, q])
            for c in range(3):
                turned[c, pl.ds(r, 8, stride=ROWS), :] = value[:, 128 * c : 128 * (c + 1)]
        ready[at, :, 0:128] = turned[0]
        ready[at, :, 128:256] = turned[1]
        ready[at, :, 256:CELLS] = turned[2, :, 0 : CELLS - 256]
        leave(at).start()
        return 0

    lax.fori_loop(0, QUADS, one, 0)

    def left(at, _):
        leave(at).wait()
        return 0

    lax.fori_loop(0, QUADS, left, 0)


def local(fields, inv_cos, coupling_lon, coupling_lat, polar_rows, bands):
    stay = functools.partial(pltpu.with_memory_space_constraint, memory_space=pltpu.HBM)
    smem, vmem, anywhere = (pl.BlockSpec(memory_space=space) for space in (pltpu.SMEM, pltpu.VMEM, pl.ANY))
    dma = pltpu.SemaphoreType.DMA
    constants = tables()
    f32, bf16 = jnp.float32, jnp.bfloat16
    pred, back = pl.pallas_call(
        kernel,
        out_shape=(
            pltpu.VMEM((ROWS, QUADS, 8, WIDE), f32),
            pltpu.VMEM((UNITS, 8, WIDE), f32),
        ),
        in_specs=[anywhere] + [smem] * 5 + [anywhere] * 4 + [vmem] * 3,
        out_specs=(vmem, vmem),
        scratch_shapes=[
            pltpu.VMEM((ROWS + 6, GROUPS, F, 8, WIDE), f32),
            pltpu.VMEM((2, GROUPS, F // 2, 8, 128), f32),
            pltpu.VMEM((2, GROUPS, F // 2, 8, 128), f32),
            pltpu.VMEM((UNITS, 8, WIDE), f32),
            pltpu.VMEM((MOST, PARTS, BLOCK, 8, WIDE), f32),
            pltpu.VMEM((MOST, PARTS, BLOCK, 8, WIDE), f32),
            pltpu.VMEM((MOST, PARTS, BLOCK, 8, WIDE), f32),
            pltpu.VMEM((BATCH, 8 * WIDE), f32),
            pltpu.VMEM((3, 2 * WIDE, 512), bf16),
            pltpu.VMEM((3, 2 * WIDE, 512), bf16),
            pltpu.VMEM((2, WIDE, 256), bf16),
            pltpu.VMEM((2, WIDE, 256), bf16),
            pltpu.VMEM((3, 2, 128, 128), f32),
            pltpu.VMEM((QUADS * 8, WIDE), f32),
            pltpu.VMEM((QUADS * 8, WIDE), f32),
            pltpu.VMEM((F * LEV * ROWS, CELLS), f32),
            dma((QUADS,)),
            dma((4,)),
            dma((2,)), dma((2,)), dma((2,)), dma((2,)),
            dma, dma((MOST,)), dma((MOST,)), dma, dma,
        ],
        compiler_params=pltpu.CompilerParams(
            collective_id=0, has_side_effects=True, vmem_limit_bytes=40 * 2**20
        ),
    )(
        stay(fields.reshape(F * LEV * ROWS, CELLS)),
        *(stay(x) for x in (inv_cos, coupling_lon, coupling_lat, polar_rows, bands)),
        *(stay(jnp.asarray(x)) for x in constants),
    )
    out = pl.pallas_call(
        place,
        out_shape=jax.ShapeDtypeStruct((QUADS, 8 * ROWS, CELLS), f32),
        in_specs=[smem, vmem, vmem],
        out_specs=anywhere,
        scratch_shapes=[
            pltpu.VMEM((3, 8 * ROWS, 128), f32),
            pltpu.VMEM((QUADS, 8 * ROWS, CELLS), f32),
            dma((QUADS,)),
        ],
        compiler_params=pltpu.CompilerParams(vmem_limit_bytes=24 * 2**20),
    )(stay(polar_rows), pred, back)
    return out.reshape(F, LEV, ROWS, CELLS)


def solution(mesh):
    return jax.shard_map(
        local,
        mesh=mesh,
        in_specs=(P(None, None, "lat", "lon"), P("lat"), P(), P(), P(), P()),
        out_specs=P(None, None, "lat", "lon"),
        check_vma=False,
    )
```
